32 devices in a mesh: row: 2 (over x), col: 16 (over z, y, core).
Axes of the slice: x: 2, y: 2, z: 4, core: 2. Of those that a mesh axis runs over, the one named last changes fastest.
Arguments:
- image: float32 [2048, 1152], P(('row', 'col'))
- text: float32 [2048, 1152], P(('row', 'col'))
- labels: int32 [2048], P(('row', 'col')), may hold values from 0 to 2047, as said below
- log_scale: float32 [1], replicated, may hold values from 2 to 2.7
- bias: float32 [1], replicated, may hold values from -10.5 to -9.5
Outputs:
- loss: float32 [1], replicated
- grad_image: float32 [2048, 1152], P(('row', 'col'))
- grad_text: float32 [2048, 1152], P(('row', 'col'))
- grad_log_scale: float32 [1], replicated
- grad_bias: float32 [1], replicated
The draws below stay inside these ranges and needn't reach their ends.
Inputs may be any that keep to these rules, and one draw needn't show every extreme that they name: `labels`: each text index 0 to 2047 appears exactly once.
All inputs are finite; a program needn't handle non-finite values.
Results may differ from the reference program's by a relative error of at most 0.0003.
Values sent between devices are 32-bit elements; how exact they have to be, the bound alone decides.
No kernel may reach another device: no remote copies, remote signals or barrier semaphores. Data moves between devices by JAX's collectives and lax.ppermute only.
A program may use at most 64 MiB of HBM per device.

```python
import math
import jax
import jax.numpy as jnp
from jax import lax

D = 1152
ROWS_DEV = 64
PAIRS = 2048
N_COL = 16


def shared_parts(key):
    order = jax.random.permutation(jax.random.fold_in(key, 101), PAIRS).astype(jnp.int32)
    row_scale = jnp.exp(jax.random.uniform(jax.random.fold_in(key, 102), (PAIRS, 1), jnp.float32) * math.log(10.0))
    col_scale = jnp.exp(jax.random.uniform(jax.random.fold_in(key, 103), (1, D), jnp.float32) * math.log(10.0)) / 3.0
    gauss = jax.random.normal(jax.random.fold_in(key, 104), (PAIRS, D), jnp.float32)
    pattern = gauss * col_scale / math.sqrt(D)
    return (order, row_scale, col_scale, pattern)


def draw_labels(key, part):
    order, row_scale, col_scale, pattern = shared_parts(key)
    return order


def draw_image(key, part):
    order, row_scale, col_scale, pattern = shared_parts(key)
    return row_scale * pattern


def draw_text(key, part):
    own = jax.random.fold_in(key, 5)
    order, row_scale, col_scale, pattern = shared_parts(key)
    reach = 3.0
    place = (jnp.arange(PAIRS, dtype=jnp.float32) / PAIRS)[:, None]
    strength = reach * place * jax.random.uniform(jax.random.fold_in(own, 1), (PAIRS, 1), jnp.float32, 0.5, 1.5)
    carried = jnp.zeros((PAIRS, D), jnp.float32).at[order].set(strength * pattern)
    text_scale = jnp.exp(jax.random.uniform(jax.random.fold_in(own, 2), (PAIRS, 1), jnp.float32) * math.log(10.0))
    noise = jax.random.normal(jax.random.fold_in(own, 3), (PAIRS, D), jnp.float32) * col_scale / math.sqrt(D)
    return text_scale * (noise + carried)


def setup_inputs(seed: int = 0) -> dict:
    key_of = jax.random.split(jax.random.key(seed), 6)
    image = draw_image(jax.random.fold_in(key_of[5], 71), 0)
    text = draw_text(jax.random.fold_in(key_of[5], 71), 0)
    labels = draw_labels(jax.random.fold_in(key_of[5], 71), 0)
    log_scale = jnp.clip(jax.random.uniform(key_of[3], (1,), jnp.float32, 2.0, 2.7), 2.0, 2.7)
    bias = jnp.clip(jax.random.uniform(key_of[4], (1,), jnp.float32, -10.5, -9.5), -10.5, -9.5)
    return dict(image=image, text=text, labels=labels, log_scale=log_scale, bias=bias)


EPSILON = 1e-06

def unit_rows(rows):
    norm = jnp.sqrt(lax.optimization_barrier(jnp.sum(rows * rows, axis=1, keepdims=True)) + EPSILON)
    return (rows / norm, norm)

def full_dot(left, right):
    return jnp.dot(left, right, precision=lax.Precision.HIGHEST, preferred_element_type=jnp.float32)

def reference(image, text, labels, log_scale, bias):
    pairs = image.shape[0]
    width = image.shape[1]
    unit_image, image_norm = unit_rows(image)
    unit_text, text_norm = unit_rows(text)
    scale = jnp.exp(log_scale[0])
    block = ROWS_DEV * N_COL
    count = pairs // block
    columns = jnp.arange(pairs, dtype=jnp.int32)
    image_blocks = unit_image.reshape(count, block, width)
    label_blocks = labels.reshape(count, block)

    def step(carry, pieces):
        grad_text_acc, loss_acc, bias_acc, scale_acc = carry
        unit_block, label_block = pieces
        cosine = full_dot(unit_block, unit_text.T)
        logit = scale * cosine + bias[0]
        positive = label_block[:, None] == columns[None, :]
        term = jnp.where(positive, jax.nn.softplus(-logit), jax.nn.softplus(logit))
        slope = jax.nn.sigmoid(logit) - positive.astype(jnp.float32)
        grad_unit = scale * full_dot(slope, unit_text)
        grad_text_acc = grad_text_acc + scale * full_dot(slope.T, unit_block)
        carry = (grad_text_acc, loss_acc + jnp.sum(term), bias_acc + jnp.sum(slope), scale_acc + jnp.sum(slope * cosine))
        return (carry, grad_unit)
    start = (jnp.zeros((pairs, width), jnp.float32), jnp.zeros((), jnp.float32), jnp.zeros((), jnp.float32), jnp.zeros((), jnp.float32))
    (unit_grad_text, summed, slope_sum, product_sum), grads = lax.scan(step, start, (image_blocks, label_blocks))
    unit_grad_image = grads.reshape(pairs, width)
    grad_image = (unit_grad_image - unit_image * lax.optimization_barrier(jnp.sum(unit_image * unit_grad_image, axis=1, keepdims=True))) / image_norm
    grad_text = (unit_grad_text - unit_text * lax.optimization_barrier(jnp.sum(unit_text * unit_grad_text, axis=1, keepdims=True))) / text_norm
    loss = (summed / pairs).reshape(1)
    grad_log_scale = (scale * product_sum / pairs).reshape(1)
    grad_bias = (slope_sum / pairs).reshape(1)
    return (loss, grad_image, grad_text, grad_log_scale, grad_bias)
```

```python
import functools

import jax
import jax.numpy as jnp
from jax import lax
from jax.experimental import pallas as pl
from jax.experimental.pallas import tpu as pltpu
from jax.sharding import PartitionSpec as P

EPSILON = 1e-06
AXES = ("row", "col")
VMEM = pl.BlockSpec(memory_space=pltpu.VMEM)
SMEM = pl.BlockSpec(memory_space=pltpu.SMEM)
VMEM_BYTES = 40 << 20


def generators(count):
    steps = []
    for bit in range(count.bit_length() - 1):
        steps.append(12 if bit == 3 else 1 << bit)
    image = steps[2::2] + steps[:1]
    text = steps[3::2] + steps[1:2]
    return image, text


def exchange(value, step, count):
    return lax.ppermute(value, AXES, [(i, i ^ step) for i in range(count)])


def spread(own, steps, count):
    blocks = {0: own}
    for step in steps:
        for mask in list(blocks):
            blocks[mask ^ step] = exchange(blocks[mask], step, count)
    return blocks


def unit_rows(rows):
    norm = jnp.sqrt(jnp.sum(rows * rows, axis=1, keepdims=True) + EPSILON)
    return rows / norm, norm


def halves(value):
    high = value.astype(jnp.bfloat16)
    low = (value - high.astype(jnp.float32)).astype(jnp.bfloat16)
    return high, low


def dot(left, right, dims):
    return lax.dot_general(left, right, (dims, ((), ())), preferred_element_type=jnp.float32)


def image_kernel(count, *refs):
    blocks, (high_ref, low_ref, label_ref) = refs[:count], refs[count:]
    rows = high_ref.shape[0] // count
    for at, block in enumerate(blocks):
        unit, _ = unit_rows(block[:rows, :])
        high, low = halves(unit)
        high_ref[pl.ds(at * rows, rows), :] = high
        low_ref[pl.ds(at * rows, rows), :] = low
    lane = lax.broadcasted_iota(jnp.int32, (8, 2 * rows), 1)
    for at in range(0, count, 2):
        first = blocks[at][pl.ds(rows, 8), pl.ds(0, 2 * rows)]
        second = blocks[at + 1][pl.ds(rows, 8), pl.ds(0, 2 * rows)]
        label_ref[:, pl.ds(at * rows, 2 * rows)] = jnp.where(lane < rows, first, second)


def tile_kernel(count, base_ref, log_scale_ref, bias_ref, high_ref, low_ref, label_ref, *refs):
    texts, outs = refs[:count], refs[count:]
    grads, (slope_ref, unit_ref, sums_ref) = outs[:count], outs[count:]
    rows = texts[0].shape[0]
    total = high_ref.shape[0]
    scale = jnp.exp(jnp.full((1, 1), log_scale_ref[0], jnp.float32))
    term_sum = jnp.zeros((1, total), jnp.float32)
    slope_sum = jnp.zeros((1, total), jnp.float32)
    product_sum = jnp.zeros((1, total), jnp.float32)
    labels = label_ref[0:1, :]
    sub = lax.broadcasted_iota(jnp.int32, (rows, total), 0)
    for at in range(count):
        unit, _ = unit_rows(texts[at][...])
        high, low = halves(unit)
        unit_ref[pl.ds(at * 3 * rows, rows), :] = high
        unit_ref[pl.ds(at * 3 * rows + rows, rows), :] = low
        unit_ref[pl.ds(at * 3 * rows + 2 * rows, rows), :] = high
        both = dot(jnp.concatenate([high, low], axis=0), high_ref[...], ((1,), (1,)))
        cosine = both[:rows] + (both[rows:] + dot(high, low_ref[...], ((1,), (1,))))
        logit = scale * cosine + bias_ref[0]
        positive = (sub + base_ref[at]).astype(jnp.float32) == labels
        decay = jnp.exp(-jnp.abs(logit))
        term = jnp.maximum(jnp.where(positive, -logit, logit), 0.0) + jnp.log1p(decay)
        sigmoid = jnp.where(logit >= 0, 1.0, decay) / (1.0 + decay)
        slope = sigmoid - positive.astype(jnp.float32)
        term_sum += jnp.sum(term, axis=0, keepdims=True)
        slope_sum += jnp.sum(slope, axis=0, keepdims=True)
        product_sum += jnp.sum(slope * cosine, axis=0, keepdims=True)
        slope_high, slope_low = halves(slope)
        both = dot(jnp.concatenate([slope_high, slope_low], axis=0), high_ref[...], ((1,), (0,)))
        grads[at][...] = both[:rows] + (both[rows:] + dot(slope_high, low_ref[...], ((1,), (0,))))
        slope_ref[pl.ds(at * 3 * rows, rows), :] = slope_high
        slope_ref[pl.ds(at * 3 * rows + rows, rows), :] = slope_high
        slope_ref[pl.ds(at * 3 * rows + 2 * rows, rows), :] = slope_low
    parts = []
    for row in (term_sum, slope_sum, product_sum):
        part = row[:, 0:128]
        for at in range(128, total, 128):
            part += row[:, at : at + 128]
        parts.append(part)
    sums_ref[...] = jnp.concatenate(parts + [jnp.zeros((5, 128), jnp.float32)], axis=0)


def tile(bases, log_scale, bias, high, low, labels, texts):
    count = len(texts)
    rows, width = texts[0].shape
    total = high.shape[0]
    out = pl.pallas_call(
        functools.partial(tile_kernel, count),
        out_shape=[jax.ShapeDtypeStruct((rows, width), jnp.float32)] * count
        + [
            jax.ShapeDtypeStruct((3 * count * rows, total), jnp.bfloat16),
            jax.ShapeDtypeStruct((3 * count * rows, width), jnp.bfloat16),
            jax.ShapeDtypeStruct((8, 128), jnp.float32),
        ],
        in_specs=[SMEM] * 3 + [VMEM] * (3 + count),
        out_specs=[VMEM] * (count + 3),
        compiler_params=pltpu.CompilerParams(vmem_limit_bytes=VMEM_BYTES),
    )(bases, log_scale, bias, high, low, labels, *texts)
    return out[:count], out[count], out[count + 1], out[count + 2]


def image_grad_kernel(slope_ref, unit_ref, *refs):
    before, (keep_ref, send_ref) = refs[:-2], refs[-2:]
    total = dot(slope_ref[...], unit_ref[...], ((0,), (0,)))
    half = keep_ref.shape[0]
    if before:
        keep_ref[...] = before[0][...] + total[:half]
        send_ref[...] = before[1][...] + total[half:]
    else:
        keep_ref[...] = total[:half]
        send_ref[...] = total[half:]


def image_grad(slope, unit, before=()):
    half, width = slope.shape[1] // 2, unit.shape[1]
    return pl.pallas_call(
        image_grad_kernel,
        out_shape=[jax.ShapeDtypeStruct((half, width), jnp.float32)] * 2,
        in_specs=[VMEM] * (2 + len(before)),
        out_specs=[VMEM] * 2,
        compiler_params=pltpu.CompilerParams(vmem_limit_bytes=VMEM_BYTES),
    )(slope, unit, *before)


def final_kernel(log_scale_ref, own_ref, *refs):
    parts, out_ref = refs[:-1], refs[-1]
    scale = jnp.exp(jnp.full((1, 1), log_scale_ref[0], jnp.float32))
    total = parts[0][...]
    for part in parts[1:]:
        total = total + part[...]
    grad = scale * total
    unit, norm = unit_rows(own_ref[...])
    out_ref[...] = (grad - unit * jnp.sum(unit * grad, axis=1, keepdims=True)) / norm


def final(log_scale, own, parts):
    return pl.pallas_call(
        final_kernel,
        out_shape=jax.ShapeDtypeStruct(own.shape, jnp.float32),
        in_specs=[SMEM] + [VMEM] * (1 + len(parts)),
        out_specs=VMEM,
        compiler_params=pltpu.CompilerParams(vmem_limit_bytes=VMEM_BYTES),
    )(log_scale, own, *parts)


def gather_back(parts, steps, count):
    parts = {mask: [part] for mask, part in parts.items()}
    for step in reversed(steps):
        masks = sorted((m for m in parts if m ^ step not in parts or m > m ^ step), reverse=True)
        masks = masks[: len(parts) // 2]
        for mask in masks:
            kept = parts.pop(mask)
            parts[mask ^ step].append(exchange(functools.reduce(jnp.add, kept), step, count))
    return parts[0]


def per_device(count, image, text, labels, log_scale, bias):
    rows, width = image.shape
    pairs = rows * count
    me = lax.axis_index("row") * lax.axis_size("col") + lax.axis_index("col")
    image_steps, text_steps = generators(count)
    label_row = jnp.tile(labels.astype(jnp.float32), 2)[None, :]
    carried = jnp.concatenate([image, jnp.pad(label_row, ((0, 7), (0, width - 2 * rows)))], axis=0)
    texts = spread(text, text_steps, count)
    images = spread(carried, image_steps, count)
    masks = list(images)
    total = rows * len(masks)
    high, low, label_lanes = pl.pallas_call(
        functools.partial(image_kernel, len(masks)),
        out_shape=[
            jax.ShapeDtypeStruct((total, width), jnp.bfloat16),
            jax.ShapeDtypeStruct((total, width), jnp.bfloat16),
            jax.ShapeDtypeStruct((8, total), jnp.float32),
        ],
        in_specs=[VMEM] * len(masks),
        out_specs=[VMEM] * 3,
        compiler_params=pltpu.CompilerParams(vmem_limit_bytes=VMEM_BYTES),
    )(*images.values())

    text_masks = list(texts)
    groups = [text_masks[:-1], text_masks[-1:]]
    grads, sums, before = {}, [], ()
    for group in groups:
        bases = jnp.stack([(me ^ mask) * rows for mask in group]).astype(jnp.int32)
        parts, slope, unit, part_sums = tile(
            bases, log_scale, bias, high, low, label_lanes, [texts[mask] for mask in group]
        )
        grads.update(zip(group, parts))
        sums.append(part_sums)
        before = image_grad(slope, unit, before)
    keep, send = before

    unit_grad_text = gather_back(grads, text_steps, count)
    received = exchange(send, image_steps[-1], count)
    kept = keep + received
    near = masks[: len(masks) // 2]
    image_parts = {mask: kept[at * rows : (at + 1) * rows] for at, mask in enumerate(near)}
    unit_grad_image = gather_back(image_parts, image_steps[:-1], count)

    scalars = functools.reduce(jnp.add, sums)
    for step in text_steps[::-1] + image_steps[::-1]:
        scalars = scalars + exchange(scalars, step, count)
    summed, slope_sum, product_sum = jnp.sum(scalars[0]), jnp.sum(scalars[1]), jnp.sum(scalars[2])

    grad_image = final(log_scale, image, unit_grad_image)
    grad_text = final(log_scale, text, unit_grad_text)
    scale = jnp.exp(log_scale[0])
    loss = (summed / pairs).reshape(1)
    grad_log_scale = (scale * product_sum / pairs).reshape(1)
    grad_bias = (slope_sum / pairs).reshape(1)
    return (loss, grad_image, grad_text, grad_log_scale, grad_bias)


def solution(mesh):
    count = mesh.shape["row"] * mesh.shape["col"]
    return jax.shard_map(
        functools.partial(per_device, count),
        mesh=mesh,
        in_specs=(P(AXES, None), P(AXES, None), P(AXES), P(), P()),
        out_specs=(P(), P(AXES, None), P(AXES, None), P(), P()),
        check_vma=False,
    )
```

```python
import functools

import jax
import jax.numpy as jnp
from jax import lax
from jax.experimental import pallas as pl
from jax.experimental.pallas import tpu as pltpu
from jax.sharding import PartitionSpec as P

EPSILON = 1e-06
LANES = 128
AXES = ("row", "col")
VMEM = pl.BlockSpec(memory_space=pltpu.VMEM)
SMEM = pl.BlockSpec(memory_space=pltpu.SMEM)
PARAMS = pltpu.CompilerParams(vmem_limit_bytes=40 << 20)
AHEAD = pl.CostEstimate(flops=10**10, bytes_accessed=10**10, transcendentals=0)


def generators(count):
    image, text = [], []
    for bit in range(1, count.bit_length() - 1):
        (text if bit in (2, 3) or bit > 4 and bit % 2 else image).append(12 if bit == 3 else 1 << bit)
    return image[::-1] + [1], text[::-1]


def exchange(value, step, count):
    return lax.ppermute(value, AXES, [(i, i ^ step) for i in range(count)])


def after(value, *others):
    return lax.optimization_barrier((value, *others))[0]


def unit_rows(rows):
    norm = jnp.sqrt(jnp.sum(rows * rows, axis=1, keepdims=True) + EPSILON)
    return rows / norm, norm


def halves(value):
    high = value.astype(jnp.bfloat16)
    low = (value - high.astype(jnp.float32)).astype(jnp.bfloat16)
    return high, low


def dot(left, right, dims):
    return lax.dot_general(left, right, (dims, ((), ())), preferred_element_type=jnp.float32)


def constants_kernel(masks, rows, me_ref, log_scale_ref, bias_ref, out_ref):
    values = [jnp.exp(jnp.full((1, LANES), log_scale_ref[0], jnp.float32))]
    values.append(jnp.full((1, LANES), bias_ref[0], jnp.float32))
    for mask in masks:
        first = jnp.bitwise_xor(me_ref[0], mask) * rows
        values.append(jnp.full((1, LANES), first, jnp.int32).astype(jnp.float32))
    values.append(jnp.zeros((out_ref.shape[0] - len(values), LANES), jnp.float32))
    out_ref[...] = jnp.concatenate(values, axis=0)


def constants(masks, rows, me, log_scale, bias):
    return pl.pallas_call(
        functools.partial(constants_kernel, masks, rows),
        out_shape=jax.ShapeDtypeStruct((len(masks) // 8 * 8 + 8, LANES), jnp.float32),
        in_specs=[SMEM] * 3,
        out_specs=VMEM,
        compiler_params=PARAMS,
    )(me, log_scale, bias)


def pack_kernel(image_ref, label_ref, out_ref):
    rows, width = image_ref.shape
    for at in range(0, width, LANES):
        out_ref[pl.ds(at // LANES * rows, rows), :] = image_ref[:, pl.ds(at, LANES)]
    label = label_ref[...].astype(jnp.float32)
    tail = jnp.broadcast_to(jnp.concatenate([label, label], axis=1), (8, LANES))
    out_ref[pl.ds(width // LANES * rows, 8), :] = tail


def pack(image, labels):
    rows, width = image.shape
    return pl.pallas_call(
        pack_kernel,
        out_shape=jax.ShapeDtypeStruct((width // LANES * rows + 8, LANES), jnp.float32),
        in_specs=[VMEM] * 2,
        out_specs=VMEM,
        compiler_params=PARAMS,
    )(image, labels.reshape(1, rows))


def image_kernel(count, *refs):
    blocks, (high_ref, low_ref, label_ref) = refs[:count], refs[count:]
    rows = high_ref.shape[0] // count
    width = high_ref.shape[1]
    for at, block in enumerate(blocks):
        squares = jnp.zeros((rows, LANES), jnp.float32)
        for piece in range(width // LANES):
            part = block[pl.ds(piece * rows, rows), :]
            squares += part * part
        norm = jnp.sqrt(jnp.sum(squares, axis=1, keepdims=True) + EPSILON)
        for piece in range(width // LANES):
            high, low = halves(block[pl.ds(piece * rows, rows), :] / norm)
            high_ref[pl.ds(at * rows, rows), pl.ds(piece * LANES, LANES)] = high
            low_ref[pl.ds(at * rows, rows), pl.ds(piece * LANES, LANES)] = low
    lane = lax.broadcasted_iota(jnp.int32, (8, LANES), 1)
    tail = pl.ds(width // LANES * rows, 8)
    for at in range(0, count, 2):
        pair = jnp.where(lane < rows, blocks[at][tail, :], blocks[at + 1][tail, :])
        label_ref[:, pl.ds(at * rows, LANES)] = pair


def image_units(blocks, rows, width):
    total = rows * len(blocks)
    return pl.pallas_call(
        functools.partial(image_kernel, len(blocks)),
        out_shape=[
            jax.ShapeDtypeStruct((total, width), jnp.bfloat16),
            jax.ShapeDtypeStruct((total, width), jnp.bfloat16),
            jax.ShapeDtypeStruct((8, total), jnp.float32),
        ],
        in_specs=[VMEM] * len(blocks),
        out_specs=[VMEM] * 3,
        compiler_params=PARAMS,
    )(*blocks)


def norm_kernel(block_ref, norm_ref):
    block = block_ref[...]
    norm = jnp.sqrt(jnp.sum(block * block, axis=1, keepdims=True) + EPSILON)
    norm_ref[...] = jnp.broadcast_to(norm, norm_ref.shape)


def row_norms(block):
    return pl.pallas_call(
        norm_kernel,
        out_shape=jax.ShapeDtypeStruct((block.shape[0], LANES), jnp.float32),
        in_specs=[VMEM],
        out_specs=VMEM,
        cost_estimate=AHEAD,
        compiler_params=PARAMS,
    )(block)


def tile_kernel(places, normed, fixed_ref, high_ref, low_ref, label_ref, *refs):
    count = len(places)
    texts, refs = refs[:count], refs[count:]
    norms, refs = dict(zip(normed, refs)), refs[len(normed) :]
    before, outs = refs[: -count - 3], refs[-count - 3 :]
    grads, (slope_ref, unit_ref, sums_ref) = outs[:count], outs[count:]
    rows = texts[0].shape[0]
    total = high_ref.shape[0]
    scale, bias = fixed_ref[0:1, 0:1], fixed_ref[1:2, 0:1]
    term_sum = jnp.zeros((1, total), jnp.float32)
    slope_sum = jnp.zeros((1, total), jnp.float32)
    product_sum = jnp.zeros((1, total), jnp.float32)
    labels = label_ref[0:1, :]
    sub = lax.broadcasted_iota(jnp.int32, (rows, total), 0).astype(jnp.float32)
    for at in range(count):
        if at in norms:
            unit = texts[at][...] / norms[at][:, 0:1]
        else:
            unit, _ = unit_rows(texts[at][...])
        high, low = halves(unit)
        unit_ref[pl.ds(at * 3 * rows, rows), :] = high
        unit_ref[pl.ds(at * 3 * rows + rows, rows), :] = low
        unit_ref[pl.ds(at * 3 * rows + 2 * rows, rows), :] = high
        both = dot(jnp.concatenate([high, low], axis=0), high_ref[...], ((1,), (1,)))
        cosine = both[:rows] + (both[rows:] + dot(high, low_ref[...], ((1,), (1,))))
        logit = scale * cosine + bias
        positive = sub + fixed_ref[2 + places[at] : 3 + places[at], 0:1] == labels
        decay = jnp.exp(-jnp.abs(logit))
        term = jnp.maximum(jnp.where(positive, -logit, logit), 0.0) + jnp.log1p(decay)
        sigmoid = jnp.where(logit >= 0, 1.0, decay) / (1.0 + decay)
        slope = sigmoid - positive.astype(jnp.float32)
        term_sum += jnp.sum(term, axis=0, keepdims=True)
        slope_sum += jnp.sum(slope, axis=0, keepdims=True)
        product_sum += jnp.sum(slope * cosine, axis=0, keepdims=True)
        slope_high, slope_low = halves(slope)
        both = dot(jnp.concatenate([slope_high, slope_low], axis=0), high_ref[...], ((1,), (0,)))
        grads[at][...] = both[:rows] + (both[rows:] + dot(slope_high, low_ref[...], ((1,), (0,))))
        slope_ref[pl.ds(at * 3 * rows, rows), :] = slope_high
        slope_ref[pl.ds(at * 3 * rows + rows, rows), :] = slope_high
        slope_ref[pl.ds(at * 3 * rows + 2 * rows, rows), :] = slope_low
    parts = []
    for row in (term_sum, slope_sum, product_sum):
        part = row[:, 0:LANES]
        for at in range(LANES, total, LANES):
            part += row[:, at : at + LANES]
        parts.append(part)
    sums = jnp.concatenate(parts + [jnp.zeros((5, LANES), jnp.float32)], axis=0)
    sums_ref[...] = before[0][...] + sums if before else sums


def tile(places, fixed, images, texts, norms, before=()):
    count = len(texts)
    rows, width = texts[0].shape
    total = images[0].shape[0]
    normed = tuple(at for at, norm in enumerate(norms) if norm is not None)
    extra = [norms[at] for at in normed] + list(before)
    out = pl.pallas_call(
        functools.partial(tile_kernel, places, normed),
        out_shape=[jax.ShapeDtypeStruct((rows, width), jnp.float32)] * count
        + [
            jax.ShapeDtypeStruct((3 * count * rows, total), jnp.bfloat16),
            jax.ShapeDtypeStruct((3 * count * rows, width), jnp.bfloat16),
            jax.ShapeDtypeStruct((8, LANES), jnp.float32),
        ],
        in_specs=[VMEM] * (4 + count + len(extra)),
        out_specs=[VMEM] * (count + 3),
        compiler_params=PARAMS,
    )(fixed, *images, *texts, *extra)
    return out[:count], out[count], out[count + 1], out[count + 2]


def image_grad_kernel(slope_ref, unit_ref, *refs):
    before, (keep_ref, send_ref) = refs[:-2], refs[-2:]
    total = dot(slope_ref[...], unit_ref[...], ((0,), (0,)))
    half = keep_ref.shape[0]
    if before:
        keep_ref[...] = before[0][...] + total[:half]
        send_ref[...] = before[1][...] + total[half:]
    else:
        keep_ref[...] = total[:half]
        send_ref[...] = total[half:]


def image_grad(slope, unit, before=()):
    half, width = slope.shape[1] // 2, unit.shape[1]
    return pl.pallas_call(
        image_grad_kernel,
        out_shape=[jax.ShapeDtypeStruct((half, width), jnp.float32)] * 2,
        in_specs=[VMEM] * (2 + len(before)),
        out_specs=[VMEM] * 2,
        compiler_params=PARAMS,
    )(slope, unit, *before)


def join_kernel(count, *refs):
    parts, others, out_ref = refs[:count], refs[count:-1], refs[-1]
    total = functools.reduce(jnp.add, [part[...] for part in parts])
    if not others:
        out_ref[...] = total
        return
    rows, width = total.shape
    for at in range(0, width, LANES):
        out_ref[pl.ds(at // LANES * rows, rows), :] = total[:, at : at + LANES]
    out_ref[pl.ds(width // LANES * rows, 8), :] = others[0][...]


def join(parts, scalars=None, cost=None):
    rows, width = parts[0].shape
    others = [] if scalars is None else [scalars]
    shape = (rows, width) if scalars is None else (width // LANES * rows + 8, LANES)
    return pl.pallas_call(
        functools.partial(join_kernel, len(parts)),
        out_shape=jax.ShapeDtypeStruct(shape, jnp.float32),
        in_specs=[VMEM] * (len(parts) + len(others)),
        out_specs=VMEM,
        cost_estimate=cost,
        compiler_params=PARAMS,
    )(*parts, *others)


def final_kernel(pairs, counts, fixed_ref, sums_ref, packed_ref, *refs):
    scale = fixed_ref[0:1, 0:1]
    ins, (image_ref, text_ref, loss_ref, scale_ref, bias_ref) = refs[:-5], refs[-5:]
    rows, width = image_ref.shape
    tail = packed_ref[pl.ds(width // LANES * rows, 8), :]
    sums = jnp.sum((sums_ref[...] + tail)[0:3, :], axis=1, keepdims=True) * (1.0 / pairs)
    loss_ref[0] = sums[0, 0]
    bias_ref[0] = sums[1, 0]
    scale_ref[0] = (scale * sums[2:3, :])[0, 0]
    pieces = [packed_ref[pl.ds(at * rows, rows), :] for at in range(width // LANES)]
    more = jnp.concatenate(pieces, axis=1)
    for own_ref, parts, out_ref in (
        (ins[0], ins[1 : 1 + counts[0]], image_ref),
        (ins[1 + counts[0]], ins[2 + counts[0] :], text_ref),
    ):
        total = functools.reduce(jnp.add, [part[...] for part in parts])
        grad = scale * (total + more if out_ref is text_ref else total)
        unit, norm = unit_rows(own_ref[...])
        out_ref[...] = (grad - unit * jnp.sum(unit * grad, axis=1, keepdims=True)) / norm


def final(pairs, fixed, scalars, packed, image, image_parts, text, text_parts):
    counts = (len(image_parts), len(text_parts))
    return pl.pallas_call(
        functools.partial(final_kernel, pairs, counts),
        out_shape=[jax.ShapeDtypeStruct(image.shape, jnp.float32)] * 2
        + [jax.ShapeDtypeStruct((1,), jnp.float32)] * 3,
        in_specs=[VMEM] * (5 + sum(counts)),
        out_specs=[VMEM] * 2 + [SMEM] * 3,
        compiler_params=PARAMS,
    )(fixed, scalars, packed, image, *image_parts, text, *text_parts)


def returns(steps):
    masks, order = [0], []
    for step in steps:
        order.insert(0, (step, [mask ^ step for mask in reversed(masks)]))
        masks += [mask ^ step for mask in masks]
    return order


def send_back(parts, step, masks, send):
    last = None
    for mask in masks:
        value = parts.pop(mask)
        value = value[0] if len(value) == 1 else join(value)
        last = send(value if last is None else after(value, last), step)
        parts[mask ^ step].append(last)


def per_device(count, image, text, labels, log_scale, bias):
    rows, width = image.shape
    pairs = rows * count
    me = lax.axis_index("row") * lax.axis_size("col") + lax.axis_index("col")
    image_steps, text_steps = generators(count)
    core = image_steps[-1]
    send = functools.partial(exchange, count=count)

    masks = [0]
    for step in text_steps:
        masks += [mask ^ step for mask in masks]
    fixed = constants(masks, rows, me.astype(jnp.int32).reshape(1), log_scale, bias)

    texts, norms = {0: text}, {}
    for step in text_steps:
        far = list(texts)[1:]
        texts[step] = send(text, step)
        for mask in far:
            norms[mask] = row_norms(texts[mask])
            texts[mask ^ step] = send(after(texts[mask], texts[step], norms[mask]), step)
    images = {0: pack(image, labels)}
    for step in image_steps[:-1]:
        far = list(images)[1:]
        images[step] = send(images[0], step)
        for mask in far:
            images[mask ^ step] = send(after(images[mask], images[step], fixed), step)
    near = list(images)
    for mask in near:
        block = images[mask]
        if mask == near[-1]:
            block = after(block, *norms.values())
        images[mask ^ core] = send(block, core)
    units = image_units(list(images.values()), rows, width)

    text_masks = list(texts)
    grads, scalars, sums = {}, (), ()
    for group in (text_masks[:-1], text_masks[-1:]):
        places = [masks.index(mask) for mask in group]
        blocks, known = [texts[mask] for mask in group], [norms.get(mask) for mask in group]
        parts, slope, unit, part = tile(places, fixed, units, blocks, known, scalars)
        grads.update(zip(group, parts))
        scalars = (part,)
        sums = image_grad(slope, unit, sums)
    keep, away = sums
    (scalars,) = scalars

    for step in [core] + image_steps[:-1]:
        scalars = scalars + send(scalars, step)
    text_parts = {mask: [part] for mask, part in grads.items()}
    for step, masks in returns(text_steps)[:-1]:
        send_back(text_parts, step, masks, send)
        scalars = after(scalars, text_parts[masks[0] ^ step][-1])
        scalars = scalars + send(scalars, step)
    packed = send(join(text_parts.pop(text_steps[0]), scalars, AHEAD), text_steps[0])
    kept = keep + send(away, core)
    image_parts = {mask: [kept[at * rows : (at + 1) * rows]] for at, mask in enumerate(near)}
    for step, masks in returns(image_steps[:-1]):
        send_back(image_parts, step, masks, send)

    grad_image, grad_text, loss, grad_log_scale, grad_bias = final(
        pairs, fixed, scalars, packed, image, image_parts[0], text, text_parts[0]
    )
    return (loss, grad_image, grad_text, grad_log_scale, grad_bias)


def solution(mesh):
    count = mesh.shape["row"] * mesh.shape["col"]
    return jax.shard_map(
        functools.partial(per_device, count),
        mesh=mesh,
        in_specs=(P(AXES, None), P(AXES, None), P(AXES), P(), P()),
        out_specs=(P(), P(AXES, None), P(AXES, None), P(), P()),
        check_vma=False,
    )
```

```python
import functools

import jax
import jax.numpy as jnp
from jax import lax
from jax.experimental import pallas as pl
from jax.experimental.pallas import tpu as pltpu
from jax.sharding import PartitionSpec as P

EPSILON = 1e-06
LANES = 128
PAD = 8
AXES = ("row", "col")
VMEM = pl.BlockSpec(memory_space=pltpu.VMEM)
SMEM = pl.BlockSpec(memory_space=pltpu.SMEM)
PARAMS = pltpu.CompilerParams(vmem_limit_bytes=40 << 20)
AHEAD = pl.CostEstimate(flops=10**10, bytes_accessed=10**10, transcendentals=0)


def generators(count):
    image, text = [], []
    for bit in range(1, count.bit_length() - 1):
        (text if bit in (2, 3) or bit > 4 and bit % 2 else image).append(12 if bit == 3 else 1 << bit)
    return image[::-1] + [1], text[::-1]


def exchange(value, step, count):
    return lax.ppermute(value, AXES, [(i, i ^ step) for i in range(count)])


def after(value, *others):
    return lax.optimization_barrier((value, *others))[0]


def unit_rows(rows):
    norm = jnp.sqrt(jnp.sum(rows * rows, axis=1, keepdims=True) + EPSILON)
    return rows / norm, norm


def halves(value):
    high = value.astype(jnp.bfloat16)
    low = (value - high.astype(jnp.float32)).astype(jnp.bfloat16)
    return high, low


def dot(left, right, dims):
    return lax.dot_general(left, right, (dims, ((), ())), preferred_element_type=jnp.float32)


def constants_kernel(masks, rows, me_ref, log_scale_ref, bias_ref, out_ref):
    values = [jnp.exp(jnp.full((1, LANES), log_scale_ref[0], jnp.float32))]
    values.append(jnp.full((1, LANES), bias_ref[0], jnp.float32))
    for mask in masks:
        first = jnp.bitwise_xor(me_ref[0], mask) * rows
        values.append(jnp.full((1, LANES), first, jnp.int32).astype(jnp.float32))
    values.append(jnp.zeros((out_ref.shape[0] - len(values), LANES), jnp.float32))
    out_ref[...] = jnp.concatenate(values, axis=0)


def constants(masks, rows, me, log_scale, bias):
    return pl.pallas_call(
        functools.partial(constants_kernel, masks, rows),
        out_shape=jax.ShapeDtypeStruct((len(masks) // 8 * 8 + 8, LANES), jnp.float32),
        in_specs=[SMEM] * 3,
        out_specs=VMEM,
        compiler_params=PARAMS,
    )(me, log_scale, bias)


def pack_kernel(image_ref, label_ref, out_ref):
    rows, width = image_ref.shape
    for at in range(0, width, LANES):
        out_ref[pl.ds(at // LANES * rows, rows), :] = image_ref[:, pl.ds(at, LANES)]
    label = label_ref[...].astype(jnp.float32)
    out_ref[pl.ds(width // LANES * rows, 1), :] = jnp.concatenate([label, label], axis=1)


def pack(image, labels):
    rows, width = image.shape
    return pl.pallas_call(
        pack_kernel,
        out_shape=jax.ShapeDtypeStruct((width // LANES * rows + 1, LANES), jnp.float32),
        in_specs=[VMEM] * 2,
        out_specs=VMEM,
        compiler_params=PARAMS,
    )(image, labels.reshape(1, rows))


def pack_text_kernel(text_ref, out_ref):
    rows, width = text_ref.shape
    for at in range(0, width, LANES):
        out_ref[pl.ds(at // LANES * rows, rows), :] = text_ref[:, pl.ds(at, LANES)]
    rest = out_ref.shape[0] - width // LANES * rows
    out_ref[pl.ds(width // LANES * rows, rest), :] = jnp.zeros((rest, LANES), jnp.float32)


def pack_text(text):
    rows, width = text.shape
    return pl.pallas_call(
        pack_text_kernel,
        out_shape=jax.ShapeDtypeStruct((width // LANES * rows + PAD, LANES), jnp.float32),
        in_specs=[VMEM],
        out_specs=VMEM,
        compiler_params=PARAMS,
    )(text)


def unpack(ref, rows):
    return jnp.concatenate([ref[pl.ds(at, rows), :] for at in range(0, ref.shape[0] // rows * rows, rows)], axis=1)


def image_kernel(count, *refs):
    blocks, (high_ref, low_ref, label_ref) = refs[:count], refs[count:]
    rows = high_ref.shape[0] // count
    width = high_ref.shape[1]
    for at, block in enumerate(blocks):
        squares = jnp.zeros((rows, LANES), jnp.float32)
        for piece in range(width // LANES):
            part = block[pl.ds(piece * rows, rows), :]
            squares += part * part
        norm = jnp.sqrt(jnp.sum(squares, axis=1, keepdims=True) + EPSILON)
        for piece in range(width // LANES):
            high, low = halves(block[pl.ds(piece * rows, rows), :] / norm)
            high_ref[pl.ds(at * rows, rows), pl.ds(piece * LANES, LANES)] = high
            low_ref[pl.ds(at * rows, rows), pl.ds(piece * LANES, LANES)] = low
    lane = lax.broadcasted_iota(jnp.int32, (1, LANES), 1)
    tail = pl.ds(width // LANES * rows, 1)
    for at in range(0, count, 2):
        pair = jnp.where(lane < rows, blocks[at][tail, :], blocks[at + 1][tail, :])
        label_ref[0:1, pl.ds(at * rows, LANES)] = pair


def image_units(blocks, rows, width):
    total = rows * len(blocks)
    return pl.pallas_call(
        functools.partial(image_kernel, len(blocks)),
        out_shape=[
            jax.ShapeDtypeStruct((total, width), jnp.bfloat16),
            jax.ShapeDtypeStruct((total, width), jnp.bfloat16),
            jax.ShapeDtypeStruct((8, total), jnp.float32),
        ],
        in_specs=[VMEM] * len(blocks),
        out_specs=[VMEM] * 3,
        compiler_params=PARAMS,
    )(*blocks)


def norm_kernel(block_ref, norm_ref):
    block = unpack(block_ref, norm_ref.shape[0])
    norm = jnp.sqrt(jnp.sum(block * block, axis=1, keepdims=True) + EPSILON)
    norm_ref[...] = jnp.broadcast_to(norm, norm_ref.shape)


def row_norms(block, rows):
    return pl.pallas_call(
        norm_kernel,
        out_shape=jax.ShapeDtypeStruct((rows, LANES), jnp.float32),
        in_specs=[VMEM],
        out_specs=VMEM,
        cost_estimate=AHEAD,
        compiler_params=PARAMS,
    )(block)


def tile_kernel(places, normed, fixed_ref, high_ref, low_ref, label_ref, *refs):
    count = len(places)
    texts, refs = refs[:count], refs[count:]
    norms, refs = dict(zip(normed, refs)), refs[len(normed) :]
    before, outs = refs[: -count - 3], refs[-count - 3 :]
    grads, (slope_ref, unit_ref, sums_ref) = outs[:count], outs[count:]
    rows = grads[0].shape[0]
    total = high_ref.shape[0]
    scale, bias = fixed_ref[0:1, 0:1], fixed_ref[1:2, 0:1]
    labels = label_ref[0:1, :]
    sub = lax.rem(lax.broadcasted_iota(jnp.int32, (count * rows, total), 0), rows).astype(jnp.float32)
    wide = count * rows
    units = []
    for at in range(count):
        if at in norms:
            units.append(halves(unpack(texts[at], rows) / norms[at][:, 0:1]))
        else:
            units.append(halves(unit_rows(unpack(texts[at], rows))[0]))
    high = jnp.concatenate([unit[0] for unit in units], axis=0)
    low = jnp.concatenate([unit[1] for unit in units], axis=0)
    unit_ref[pl.ds(0, wide), :] = high
    unit_ref[pl.ds(wide, wide), :] = low
    unit_ref[pl.ds(2 * wide, wide), :] = high
    both = dot(jnp.concatenate([high, low], axis=0), high_ref[...], ((1,), (1,)))
    cosine = both[:wide] + (both[wide:] + dot(high, low_ref[...], ((1,), (1,))))
    logit = scale * cosine + bias
    first = [jnp.broadcast_to(fixed_ref[2 + place : 3 + place, 0:1], (rows, 1)) for place in places]
    positive = sub + jnp.concatenate(first, axis=0) == labels
    decay = jnp.exp(-jnp.abs(logit))
    term = jnp.maximum(jnp.where(positive, -logit, logit), 0.0) + jnp.log1p(decay)
    sigmoid = jnp.where(logit >= 0, 1.0, decay) / (1.0 + decay)
    slope = sigmoid - positive.astype(jnp.float32)
    term_sum = jnp.sum(term, axis=0, keepdims=True)
    slope_sum = jnp.sum(slope, axis=0, keepdims=True)
    product_sum = jnp.sum(slope * cosine, axis=0, keepdims=True)
    slope_high, slope_low = halves(slope)
    both = dot(jnp.concatenate([slope_high, slope_low], axis=0), high_ref[...], ((1,), (0,)))
    both = both[:wide] + (both[wide:] + dot(slope_high, low_ref[...], ((1,), (0,))))
    for at in range(count):
        grads[at][...] = both[at * rows : (at + 1) * rows]
    slope_ref[pl.ds(0, wide), :] = slope_high
    slope_ref[pl.ds(wide, wide), :] = slope_high
    slope_ref[pl.ds(2 * wide, wide), :] = slope_low
    parts = []
    for row in (term_sum, slope_sum, product_sum):
        part = row[:, 0:LANES]
        for at in range(LANES, total, LANES):
            part += row[:, at : at + LANES]
        parts.append(part)
    sums = jnp.concatenate(parts + [jnp.zeros((5, LANES), jnp.float32)], axis=0)
    sums_ref[...] = before[0][...] + sums if before else sums


def tile(rows, width, places, fixed, images, texts, norms, before=()):
    count = len(texts)
    total = images[0].shape[0]
    normed = tuple(at for at, norm in enumerate(norms) if norm is not None)
    extra = [norms[at] for at in normed] + list(before)
    out = pl.pallas_call(
        functools.partial(tile_kernel, places, normed),
        out_shape=[jax.ShapeDtypeStruct((rows, width), jnp.float32)] * count
        + [
            jax.ShapeDtypeStruct((3 * count * rows, total), jnp.bfloat16),
            jax.ShapeDtypeStruct((3 * count * rows, width), jnp.bfloat16),
            jax.ShapeDtypeStruct((8, LANES), jnp.float32),
        ],
        in_specs=[VMEM] * (4 + count + len(extra)),
        out_specs=[VMEM] * (count + 3),
        compiler_params=PARAMS,
    )(fixed, *images, *texts, *extra)
    return out[:count], out[count], out[count + 1], out[count + 2]


def image_grad_kernel(slope_ref, unit_ref, *refs):
    before, (keep_ref, send_ref) = refs[:-2], refs[-2:]
    total = dot(slope_ref[...], unit_ref[...], ((0,), (0,)))
    half = keep_ref.shape[0]
    if before:
        keep_ref[...] = before[0][...] + total[:half]
        send_ref[...] = before[1][...] + total[half:]
    else:
        keep_ref[...] = total[:half]
        send_ref[...] = total[half:]


def image_grad(slope, unit, before=()):
    half, width = slope.shape[1] // 2, unit.shape[1]
    return pl.pallas_call(
        image_grad_kernel,
        out_shape=[jax.ShapeDtypeStruct((half, width), jnp.float32)] * 2,
        in_specs=[VMEM] * (2 + len(before)),
        out_specs=[VMEM] * 2,
        compiler_params=PARAMS,
    )(slope, unit, *before)


def join_kernel(count, *refs):
    parts, others, out_ref = refs[:count], refs[count:-1], refs[-1]
    total = functools.reduce(jnp.add, [part[...] for part in parts])
    if not others:
        out_ref[...] = total
        return
    rows, width = total.shape
    for at in range(0, width, LANES):
        out_ref[pl.ds(at // LANES * rows, rows), :] = total[:, at : at + LANES]
    out_ref[pl.ds(width // LANES * rows, 8), :] = others[0][...]


def join(parts, scalars=None, cost=None):
    rows, width = parts[0].shape
    others = [] if scalars is None else [scalars]
    shape = (rows, width) if scalars is None else (width // LANES * rows + 8, LANES)
    return pl.pallas_call(
        functools.partial(join_kernel, len(parts)),
        out_shape=jax.ShapeDtypeStruct(shape, jnp.float32),
        in_specs=[VMEM] * (len(parts) + len(others)),
        out_specs=VMEM,
        cost_estimate=cost,
        compiler_params=PARAMS,
    )(*parts, *others)


def final_kernel(pairs, counts, fixed_ref, sums_ref, *refs):
    scale = fixed_ref[0:1, 0:1]
    ins, (image_ref, text_ref, loss_ref, scale_ref, bias_ref) = refs[:-5], refs[-5:]
    sums = jnp.sum(sums_ref[0:3, :], axis=1, keepdims=True) * (1.0 / pairs)
    loss_ref[0] = sums[0, 0]
    bias_ref[0] = sums[1, 0]
    scale_ref[0] = (scale * sums[2:3, :])[0, 0]
    for own_ref, parts, out_ref in (
        (ins[0], ins[1 : 1 + counts[0]], image_ref),
        (ins[1 + counts[0]], ins[2 + counts[0] :], text_ref),
    ):
        total = functools.reduce(jnp.add, [part[...] for part in parts])
        grad = scale * total
        unit, norm = unit_rows(own_ref[...])
        out_ref[...] = (grad - unit * jnp.sum(unit * grad, axis=1, keepdims=True)) / norm


def final(pairs, fixed, scalars, image, image_parts, text, text_parts):
    counts = (len(image_parts), len(text_parts))
    return pl.pallas_call(
        functools.partial(final_kernel, pairs, counts),
        out_shape=[jax.ShapeDtypeStruct(image.shape, jnp.float32)] * 2
        + [jax.ShapeDtypeStruct((1,), jnp.float32)] * 3,
        in_specs=[VMEM] * (4 + sum(counts)),
        out_specs=[VMEM] * 2 + [SMEM] * 3,
        compiler_params=PARAMS,
    )(fixed, scalars, image, *image_parts, text, *text_parts)


def returns(steps):
    masks, order = [0], []
    for step in steps:
        order.insert(0, (step, [mask ^ step for mask in reversed(masks)]))
        masks += [mask ^ step for mask in masks]
    return order


def send_back(parts, step, masks, send):
    last = None
    for mask in masks:
        value = parts.pop(mask)
        value = value[0] if len(value) == 1 else join(value)
        last = send(value if last is None else after(value, last), step)
        parts[mask ^ step].append(last)


def per_device(count, image, text, labels, log_scale, bias):
    rows, width = image.shape
    pairs = rows * count
    me = lax.axis_index("row") * lax.axis_size("col") + lax.axis_index("col")
    image_steps, text_steps = generators(count)
    core = image_steps[-1]
    send = functools.partial(exchange, count=count)

    masks = [0]
    for step in text_steps:
        masks += [mask ^ step for mask in masks]
    fixed = constants(masks, rows, me.astype(jnp.int32).reshape(1), log_scale, bias)

    texts, norms = {0: pack_text(text)}, {}
    for step in text_steps:
        far = list(texts)[1:]
        texts[step] = send(texts[0], step)
        for mask in far:
            norms[mask] = row_norms(texts[mask], rows)
            texts[mask ^ step] = send(after(texts[mask], texts[step], norms[mask]), step)
    images = {0: pack(image, labels)}
    for step in image_steps[:-1]:
        far = list(images)[1:]
        images[step] = send(images[0], step)
        for mask in far:
            images[mask ^ step] = send(after(images[mask], images[step], fixed), step)
    near = list(images)
    for mask in near:
        block = images[mask]
        if mask == near[-1]:
            block = after(block, *norms.values())
        images[mask ^ core] = send(block, core)
    units = image_units(list(images.values()), rows, width)

    text_masks = list(texts)
    grads, scalars, sums = {}, (), ()
    for group in (text_masks[:-1], text_masks[-1:]):
        places = [masks.index(mask) for mask in group]
        blocks, known = [texts[mask] for mask in group], [norms.get(mask) for mask in group]
        parts, slope, unit, part = tile(rows, width, places, fixed, units, blocks, known, scalars)
        grads.update(zip(group, parts))
        scalars = (part,)
        sums = image_grad(slope, unit, sums)
    keep, away = sums
    (scalars,) = scalars

    for step in text_steps[::-1]:
        scalars = join([scalars, send(scalars, step)], cost=AHEAD)
    text_parts = {mask: [part] for mask, part in grads.items()}
    order = returns(text_steps)
    for step, masks in order[:-1]:
        send_back(text_parts, step, masks, send)
    far = join(text_parts.pop(text_steps[0]))
    scalars = after(scalars, far)
    text_parts[0].append(send(far, text_steps[0]))
    kept = keep + send(away, core)
    image_parts = {mask: [kept[at * rows : (at + 1) * rows]] for at, mask in enumerate(near)}
    for step, masks in returns(image_steps[:-1]):
        send_back(image_parts, step, masks, send)
    for step in image_steps[::-1]:
        scalars = scalars + send(scalars, step)

    grad_image, grad_text, loss, grad_log_scale, grad_bias = final(
        pairs, fixed, scalars, image, image_parts[0], text, text_parts[0]
    )
    return (loss, grad_image, grad_text, grad_log_scale, grad_bias)


def solution(mesh):
    count = mesh.shape["row"] * mesh.shape["col"]
    return jax.shard_map(
        functools.partial(per_device, count),
        mesh=mesh,
        in_specs=(P(AXES, None), P(AXES, None), P(AXES), P(), P()),
        out_specs=(P(), P(AXES, None), P(AXES, None), P(), P()),
        check_vma=False,
    )
```

```python
import functools

import jax
import jax.numpy as jnp
from jax import lax
from jax.experimental import pallas as pl
from jax.experimental.pallas import tpu as pltpu
from jax.sharding import PartitionSpec as P

EPSILON = 1e-06
LANES = 128
PAD = 8
AXES = ("row", "col")
VMEM = pl.BlockSpec(memory_space=pltpu.VMEM)
SMEM = pl.BlockSpec(memory_space=pltpu.SMEM)
PARAMS = pltpu.CompilerParams(vmem_limit_bytes=40 << 20)
AHEAD = pl.CostEstimate(flops=10**10, bytes_accessed=10**10, transcendentals=0)


def generators(count):
    image, text = [], []
    for bit in range(1, count.bit_length() - 1):
        (text if bit in (2, 3) or bit > 4 and bit % 2 else image).append(1 << bit)
    return image + [1], text[::-1]


def exchange(value, step, count):
    return lax.ppermute(value, AXES, [(i, i ^ step) for i in range(count)])


def after(value, *others):
    return lax.optimization_barrier((value, *others))[0]


def unit_rows(rows):
    norm = jnp.sqrt(jnp.sum(rows * rows, axis=1, keepdims=True) + EPSILON)
    return rows / norm, norm


def halves(value):
    high = value.astype(jnp.bfloat16)
    low = (value - high.astype(jnp.float32)).astype(jnp.bfloat16)
    return high, low


def dot(left, right, dims):
    return lax.dot_general(left, right, (dims, ((), ())), preferred_element_type=jnp.float32)


def constants_kernel(masks, rows, me_ref, log_scale_ref, bias_ref, out_ref):
    values = [jnp.exp(jnp.full((1, LANES), log_scale_ref[0], jnp.float32))]
    values.append(jnp.full((1, LANES), bias_ref[0], jnp.float32))
    for mask in masks:
        first = jnp.bitwise_xor(me_ref[0], mask) * rows
        values.append(jnp.full((1, LANES), first, jnp.int32).astype(jnp.float32))
    values.append(jnp.zeros((out_ref.shape[0] - len(values), LANES), jnp.float32))
    out_ref[...] = jnp.concatenate(values, axis=0)


def constants(masks, rows, me, log_scale, bias):
    return pl.pallas_call(
        functools.partial(constants_kernel, masks, rows),
        out_shape=jax.ShapeDtypeStruct((len(masks) // 8 * 8 + 8, LANES), jnp.float32),
        in_specs=[SMEM] * 3,
        out_specs=VMEM,
        compiler_params=PARAMS,
    )(me, log_scale, bias)


def pack_kernel(image_ref, text_ref, label_ref, image_out, text_out, image, text, labels, sems):
    rows, width = image_ref.shape
    moves = [(text_ref, text), (image_ref, image), (label_ref, labels)]
    copies = [pltpu.make_async_copy(*move, sems.at[at]) for at, move in enumerate(moves)]
    for copy in copies:
        copy.start()
    text_out[pl.ds(width // LANES * rows, PAD), :] = jnp.zeros((PAD, LANES), jnp.float32)
    for copy, held, out in zip(copies, (text, image), (text_out, image_out)):
        copy.wait()
        for at in range(0, width, LANES):
            out[pl.ds(at // LANES * rows, rows), :] = held[:, pl.ds(at, LANES)]
    copies[2].wait()
    label = labels[...].astype(jnp.float32)
    image_out[pl.ds(width // LANES * rows, 1), :] = jnp.concatenate([label, label], axis=1)


def pack(image, text, labels):
    rows, width = image.shape
    pieces = width // LANES * rows
    return pl.pallas_call(
        pack_kernel,
        out_shape=[jax.ShapeDtypeStruct((pieces + more, LANES), jnp.float32) for more in (1, PAD)],
        in_specs=[pl.BlockSpec(memory_space=pltpu.HBM)] * 3,
        out_specs=[VMEM] * 2,
        scratch_shapes=[
            pltpu.VMEM((rows, width), jnp.float32),
            pltpu.VMEM((rows, width), jnp.float32),
            pltpu.VMEM((1, rows), jnp.int32),
            pltpu.SemaphoreType.DMA((3,)),
        ],
        compiler_params=pltpu.CompilerParams(vmem_limit_bytes=60 << 20),
    )(image, text, labels.reshape(1, rows))


def unpack(ref, rows):
    return jnp.concatenate([ref[pl.ds(at, rows), :] for at in range(0, ref.shape[0] // rows * rows, rows)], axis=1)


def image_kernel(count, *refs):
    blocks, (high_ref, low_ref, label_ref) = refs[:count], refs[count:]
    rows = high_ref.shape[0] // count
    width = high_ref.shape[1]
    for at, block in enumerate(blocks):
        squares = jnp.zeros((rows, LANES), jnp.float32)
        for piece in range(width // LANES):
            part = block[pl.ds(piece * rows, rows), :]
            squares += part * part
        norm = jnp.sqrt(jnp.sum(squares, axis=1, keepdims=True) + EPSILON)
        for piece in range(width // LANES):
            high, low = halves(block[pl.ds(piece * rows, rows), :] / norm)
            high_ref[pl.ds(at * rows, rows), pl.ds(piece * LANES, LANES)] = high
            low_ref[pl.ds(at * rows, rows), pl.ds(piece * LANES, LANES)] = low
    lane = lax.broadcasted_iota(jnp.int32, (1, LANES), 1)
    tail = pl.ds(width // LANES * rows, 1)
    for at in range(0, count, 2):
        pair = jnp.where(lane < rows, blocks[at][tail, :], blocks[at + 1][tail, :])
        label_ref[0:1, pl.ds(at * rows, LANES)] = pair


def image_units(blocks, rows, width):
    total = rows * len(blocks)
    return pl.pallas_call(
        functools.partial(image_kernel, len(blocks)),
        out_shape=[
            jax.ShapeDtypeStruct((total, width), jnp.bfloat16),
            jax.ShapeDtypeStruct((total, width), jnp.bfloat16),
            jax.ShapeDtypeStruct((8, total), jnp.float32),
        ],
        in_specs=[VMEM] * len(blocks),
        out_specs=[VMEM] * 3,
        compiler_params=PARAMS,
    )(*blocks)


def norm_kernel(block_ref, norm_ref):
    block = unpack(block_ref, norm_ref.shape[0])
    norm = jnp.sqrt(jnp.sum(block * block, axis=1, keepdims=True) + EPSILON)
    norm_ref[...] = jnp.broadcast_to(norm, norm_ref.shape)


def row_norms(block, rows):
    return pl.pallas_call(
        norm_kernel,
        out_shape=jax.ShapeDtypeStruct((rows, LANES), jnp.float32),
        in_specs=[VMEM],
        out_specs=VMEM,
        cost_estimate=AHEAD,
        compiler_params=PARAMS,
    )(block)


def tile_kernel(places, normed, fixed_ref, high_ref, low_ref, label_ref, *refs):
    count = len(places)
    texts, refs = refs[:count], refs[count:]
    norms, refs = dict(zip(normed, refs)), refs[len(normed) :]
    before, outs = refs[: -count - 3], refs[-count - 3 :]
    grads, (slope_ref, unit_ref, sums_ref) = outs[:count], outs[count:]
    rows = grads[0].shape[0]
    total = high_ref.shape[0]
    scale, bias = fixed_ref[0:1, 0:1], fixed_ref[1:2, 0:1]
    labels = label_ref[0:1, :]
    sub = lax.rem(lax.broadcasted_iota(jnp.int32, (count * rows, total), 0), rows).astype(jnp.float32)
    wide = count * rows
    units = []
    for at in range(count):
        if at in norms:
            units.append(halves(unpack(texts[at], rows) / norms[at][:, 0:1]))
        else:
            units.append(halves(unit_rows(unpack(texts[at], rows))[0]))
    high = jnp.concatenate([unit[0] for unit in units], axis=0)
    low = jnp.concatenate([unit[1] for unit in units], axis=0)
    unit_ref[pl.ds(0, wide), :] = high
    unit_ref[pl.ds(wide, wide), :] = low
    unit_ref[pl.ds(2 * wide, wide), :] = high
    both = dot(jnp.concatenate([high, low], axis=0), high_ref[...], ((1,), (1,)))
    cosine = both[:wide] + (both[wide:] + dot(high, low_ref[...], ((1,), (1,))))
    logit = scale * cosine + bias
    first = [jnp.broadcast_to(fixed_ref[2 + place : 3 + place, 0:1], (rows, 1)) for place in places]
    positive = sub + jnp.concatenate(first, axis=0) == labels
    decay = jnp.exp(-jnp.abs(logit))
    term = jnp.maximum(jnp.where(positive, -logit, logit), 0.0) + jnp.log1p(decay)
    sigmoid = jnp.where(logit >= 0, 1.0, decay) / (1.0 + decay)
    slope = sigmoid - positive.astype(jnp.float32)
    term_sum = jnp.sum(term, axis=0, keepdims=True)
    slope_sum = jnp.sum(slope, axis=0, keepdims=True)
    product_sum = jnp.sum(slope * cosine, axis=0, keepdims=True)
    slope_high, slope_low = halves(slope)
    both = dot(jnp.concatenate([slope_high, slope_low], axis=0), high_ref[...], ((1,), (0,)))
    both = both[:wide] + (both[wide:] + dot(slope_high, low_ref[...], ((1,), (0,))))
    for at in range(count):
        grads[at][...] = both[at * rows : (at + 1) * rows]
    slope_ref[pl.ds(0, wide), :] = slope_high
    slope_ref[pl.ds(wide, wide), :] = slope_high
    slope_ref[pl.ds(2 * wide, wide), :] = slope_low
    parts = []
    for row in (term_sum, slope_sum, product_sum):
        part = row[:, 0:LANES]
        for at in range(LANES, total, LANES):
            part += row[:, at : at + LANES]
        parts.append(part)
    sums = jnp.concatenate(parts + [jnp.zeros((5, LANES), jnp.float32)], axis=0)
    sums_ref[...] = before[0][...] + sums if before else sums


def tile(rows, width, places, fixed, images, texts, norms, before=()):
    count = len(texts)
    total = images[0].shape[0]
    normed = tuple(at for at, norm in enumerate(norms) if norm is not None)
    extra = [norms[at] for at in normed] + list(before)
    out = pl.pallas_call(
        functools.partial(tile_kernel, places, normed),
        out_shape=[jax.ShapeDtypeStruct((rows, width), jnp.float32)] * count
        + [
            jax.ShapeDtypeStruct((3 * count * rows, total), jnp.bfloat16),
            jax.ShapeDtypeStruct((3 * count * rows, width), jnp.bfloat16),
            jax.ShapeDtypeStruct((8, LANES), jnp.float32),
        ],
        in_specs=[VMEM] * (4 + count + len(extra)),
        out_specs=[VMEM] * (count + 3),
        compiler_params=PARAMS,
    )(fixed, *images, *texts, *extra)
    return out[:count], out[count], out[count + 1], out[count + 2]


def image_grad_kernel(slope_ref, unit_ref, *refs):
    before, (keep_ref, send_ref) = refs[:-2], refs[-2:]
    total = dot(slope_ref[...], unit_ref[...], ((0,), (0,)))
    half = keep_ref.shape[0]
    if before:
        keep_ref[...] = before[0][...] + total[:half]
        send_ref[...] = before[1][...] + total[half:]
    else:
        keep_ref[...] = total[:half]
        send_ref[...] = total[half:]


def image_grad(slope, unit, before=()):
    half, width = slope.shape[1] // 2, unit.shape[1]
    return pl.pallas_call(
        image_grad_kernel,
        out_shape=[jax.ShapeDtypeStruct((half, width), jnp.float32)] * 2,
        in_specs=[VMEM] * (2 + len(before)),
        out_specs=[VMEM] * 2,
        compiler_params=PARAMS,
    )(slope, unit, *before)


def join_kernel(count, *refs):
    parts, others, out_ref = refs[:count], refs[count:-1], refs[-1]
    total = functools.reduce(jnp.add, [part[...] for part in parts])
    if not others:
        out_ref[...] = total
        return
    rows, width = total.shape
    for at in range(0, width, LANES):
        out_ref[pl.ds(at // LANES * rows, rows), :] = total[:, at : at + LANES]
    out_ref[pl.ds(width // LANES * rows, 8), :] = others[0][...]


def join(parts, scalars=None, cost=None):
    rows, width = parts[0].shape
    others = [] if scalars is None else [scalars]
    shape = (rows, width) if scalars is None else (width // LANES * rows + 8, LANES)
    return pl.pallas_call(
        functools.partial(join_kernel, len(parts)),
        out_shape=jax.ShapeDtypeStruct(shape, jnp.float32),
        in_specs=[VMEM] * (len(parts) + len(others)),
        out_specs=VMEM,
        cost_estimate=cost,
        compiler_params=PARAMS,
    )(*parts, *others)


def final_kernel(pairs, counts, fixed_ref, sums_ref, *refs):
    scale = fixed_ref[0:1, 0:1]
    ins, (image_ref, text_ref, loss_ref, scale_ref, bias_ref) = refs[:-5], refs[-5:]
    sums = jnp.sum(sums_ref[0:3, :], axis=1, keepdims=True) * (1.0 / pairs)
    loss_ref[0] = sums[0, 0]
    bias_ref[0] = sums[1, 0]
    scale_ref[0] = (scale * sums[2:3, :])[0, 0]
    for own_ref, parts, out_ref in (
        (ins[0], ins[1 : 1 + counts[0]], image_ref),
        (ins[1 + counts[0]], ins[2 + counts[0] :], text_ref),
    ):
        total = functools.reduce(jnp.add, [part[...] for part in parts])
        grad = scale * total
        unit, norm = unit_rows(own_ref[...])
        out_ref[...] = (grad - unit * jnp.sum(unit * grad, axis=1, keepdims=True)) / norm


def final(pairs, fixed, scalars, image, image_parts, text, text_parts):
    counts = (len(image_parts), len(text_parts))
    return pl.pallas_call(
        functools.partial(final_kernel, pairs, counts),
        out_shape=[jax.ShapeDtypeStruct(image.shape, jnp.float32)] * 2
        + [jax.ShapeDtypeStruct((1,), jnp.float32)] * 3,
        in_specs=[VMEM] * (4 + sum(counts)),
        out_specs=[VMEM] * 2 + [SMEM] * 3,
        compiler_params=PARAMS,
    )(fixed, scalars, image, *image_parts, text, *text_parts)


def returns(steps):
    masks, order = [0], []
    for step in steps:
        order.insert(0, (step, [mask ^ step for mask in reversed(masks)]))
        masks += [mask ^ step for mask in masks]
    return order


def send_back(parts, step, masks, send):
    last = None
    for mask in masks:
        value = parts.pop(mask)
        value = value[0] if len(value) == 1 else join(value)
        last = send(value if last is None else after(value, last), step)
        parts[mask ^ step].append(last)


def per_device(count, image, text, labels, log_scale, bias):
    rows, width = image.shape
    pairs = rows * count
    me = lax.axis_index("row") * lax.axis_size("col") + lax.axis_index("col")
    image_steps, text_steps = generators(count)
    core = image_steps[-1]
    send = functools.partial(exchange, count=count)

    masks = [0]
    for step in text_steps:
        masks += [mask ^ step for mask in masks]
    fixed = constants(masks, rows, me.astype(jnp.int32).reshape(1), log_scale, bias)

    packed_image, packed_text = pack(image, text, labels)
    texts, norms = {0: packed_text}, {}
    for step in text_steps:
        far = list(texts)[1:]
        texts[step] = send(texts[0], step)
        for mask in far:
            norms[mask] = row_norms(texts[mask], rows)
            texts[mask ^ step] = send(after(texts[mask], norms[mask]), step)
    images = {0: packed_image}
    for step in image_steps[:-1]:
        far = list(images)[1:]
        images[step] = send(images[0], step)
        for mask in far:
            images[mask ^ step] = send(after(images[mask], fixed), step)
    near = list(images)
    for mask in near:
        block = images[mask]
        if mask == near[-1]:
            block = after(block, *norms.values(), *(texts[step] for step in text_steps))
        images[mask ^ core] = send(block, core)
    units = image_units(list(images.values()), rows, width)

    text_masks = list(texts)
    grads, scalars, sums = {}, (), ()
    for group in (text_masks[:-1], text_masks[-1:]):
        places = [masks.index(mask) for mask in group]
        blocks, known = [texts[mask] for mask in group], [norms.get(mask) for mask in group]
        parts, slope, unit, part = tile(rows, width, places, fixed, units, blocks, known, scalars)
        grads.update(zip(group, parts))
        scalars = (part,)
        sums = image_grad(slope, unit, sums)
    keep, away = sums
    (scalars,) = scalars

    for step in text_steps[:0:-1]:
        scalars = join([scalars, send(scalars, step)], cost=AHEAD)
    scalars = scalars + send(scalars, core)
    scalars = join([scalars, send(scalars, text_steps[0])], cost=AHEAD)

    text_parts = {mask: [part] for mask, part in grads.items()}
    order = returns(text_steps)
    for step, masks in order[:-1]:
        send_back(text_parts, step, masks, send)
    far = join(text_parts.pop(text_steps[0]))
    scalars = after(scalars, far)
    text_parts[0].append(send(far, text_steps[0]))
    kept = keep + send(away, core)
    image_parts = {mask: [kept[at * rows : (at + 1) * rows]] for at, mask in enumerate(near)}
    for step, masks in returns(image_steps[:-1]):
        send_back(image_parts, step, masks, send)
    for step in image_steps[-2::-1]:
        scalars = scalars + send(scalars, step)

    grad_image, grad_text, loss, grad_log_scale, grad_bias = final(
        pairs, fixed, scalars, image, image_parts[0], text, text_parts[0]
    )
    return (loss, grad_image, grad_text, grad_log_scale, grad_bias)


def solution(mesh):
    count = mesh.shape["row"] * mesh.shape["col"]
    return jax.shard_map(
        functools.partial(per_device, count),
        mesh=mesh,
        in_specs=(P(AXES, None), P(AXES, None), P(AXES), P(), P()),
        out_specs=(P(), P(AXES, None), P(AXES, None), P(), P()),
        check_vma=False,
    )
```

```python
import functools

import jax
import jax.numpy as jnp
from jax import lax
from jax.experimental import pallas as pl
from jax.experimental.pallas import tpu as pltpu
from jax.sharding import PartitionSpec as P

EPSILON = 1e-06
LANES = 128
PAD = 8
AXES = ("row", "col")
VMEM = pl.BlockSpec(memory_space=pltpu.VMEM)
SMEM = pl.BlockSpec(memory_space=pltpu.SMEM)
PARAMS = pltpu.CompilerParams(vmem_limit_bytes=40 << 20)
AHEAD = pl.CostEstimate(flops=10**10, bytes_accessed=10**10, transcendentals=0)


def generators(count):
    image, text = [], []
    for bit in range(1, count.bit_length() - 1):
        (text if bit in (2, 3) or bit > 4 and bit % 2 else image).append(1 << bit)
    return image + [1], text[::-1]


def exchange(value, step, count):
    return lax.ppermute(value, AXES, [(i, i ^ step) for i in range(count)])


def after(value, *others):
    return lax.optimization_barrier((value, *others))[0]


def unit_rows(rows):
    norm = jnp.sqrt(jnp.sum(rows * rows, axis=1, keepdims=True) + EPSILON)
    return rows / norm, norm


def halves(value):
    high = value.astype(jnp.bfloat16)
    low = (value - high.astype(jnp.float32)).astype(jnp.bfloat16)
    return high, low


def dot(left, right, dims):
    return lax.dot_general(left, right, (dims, ((), ())), preferred_element_type=jnp.float32)


def constants_kernel(masks, rows, me_ref, log_scale_ref, bias_ref, out_ref):
    values = [jnp.exp(jnp.full((1, LANES), log_scale_ref[0], jnp.float32))]
    values.append(jnp.full((1, LANES), bias_ref[0], jnp.float32))
    for mask in masks:
        first = jnp.bitwise_xor(me_ref[0], mask) * rows
        values.append(jnp.full((1, LANES), first, jnp.int32).astype(jnp.float32))
    values.append(jnp.zeros((out_ref.shape[0] - len(values), LANES), jnp.float32))
    out_ref[...] = jnp.concatenate(values, axis=0)


def constants(masks, rows, me, log_scale, bias):
    return pl.pallas_call(
        functools.partial(constants_kernel, masks, rows),
        out_shape=jax.ShapeDtypeStruct((len(masks) // 8 * 8 + 8, LANES), jnp.float32),
        in_specs=[SMEM] * 3,
        out_specs=VMEM,
        compiler_params=PARAMS,
    )(me, log_scale, bias)


def pack_kernel(image_ref, text_ref, label_ref, image_out, text_out, image, text, labels, sems):
    rows, width = image_ref.shape
    moves = [(text_ref, text), (image_ref, image), (label_ref, labels)]
    copies = [pltpu.make_async_copy(*move, sems.at[at]) for at, move in enumerate(moves)]
    for copy in copies:
        copy.start()
    text_out[pl.ds(width // LANES * rows, PAD), :] = jnp.zeros((PAD, LANES), jnp.float32)
    for copy, held, out in zip(copies, (text, image), (text_out, image_out)):
        copy.wait()
        for at in range(0, width, LANES):
            out[pl.ds(at // LANES * rows, rows), :] = held[:, pl.ds(at, LANES)]
    copies[2].wait()
    label = labels[...].astype(jnp.float32)
    image_out[pl.ds(width // LANES * rows, 1), :] = jnp.concatenate([label, label], axis=1)


def pack(image, text, labels):
    rows, width = image.shape
    pieces = width // LANES * rows
    return pl.pallas_call(
        pack_kernel,
        out_shape=[jax.ShapeDtypeStruct((pieces + more, LANES), jnp.float32) for more in (1, PAD)],
        in_specs=[pl.BlockSpec(memory_space=pltpu.HBM)] * 3,
        out_specs=[VMEM] * 2,
        scratch_shapes=[
            pltpu.VMEM((rows, width), jnp.float32),
            pltpu.VMEM((rows, width), jnp.float32),
            pltpu.VMEM((1, rows), jnp.int32),
            pltpu.SemaphoreType.DMA((3,)),
        ],
        compiler_params=pltpu.CompilerParams(vmem_limit_bytes=60 << 20),
    )(image, text, labels.reshape(1, rows))


def unpack(ref, rows):
    return jnp.concatenate([ref[pl.ds(at, rows), :] for at in range(0, ref.shape[0] // rows * rows, rows)], axis=1)


def image_units(blocks, high_ref, low_ref, label_ref):
    count = len(blocks)
    rows = high_ref.shape[0] // count
    width = high_ref.shape[1]
    for at, block in enumerate(blocks):
        squares = jnp.zeros((rows, LANES), jnp.float32)
        for piece in range(width // LANES):
            part = block[pl.ds(piece * rows, rows), :]
            squares += part * part
        norm = jnp.sqrt(jnp.sum(squares, axis=1, keepdims=True) + EPSILON)
        for piece in range(width // LANES):
            high, low = halves(block[pl.ds(piece * rows, rows), :] / norm)
            high_ref[pl.ds(at * rows, rows), pl.ds(piece * LANES, LANES)] = high
            low_ref[pl.ds(at * rows, rows), pl.ds(piece * LANES, LANES)] = low
    lane = lax.broadcasted_iota(jnp.int32, (1, LANES), 1)
    tail = pl.ds(width // LANES * rows, 1)
    for at in range(0, count, 2):
        pair = jnp.where(lane < rows, blocks[at][tail, :], blocks[at + 1][tail, :])
        label_ref[0:1, pl.ds(at * rows, LANES)] = pair


def norm_kernel(block_ref, norm_ref):
    block = unpack(block_ref, norm_ref.shape[0])
    norm = jnp.sqrt(jnp.sum(block * block, axis=1, keepdims=True) + EPSILON)
    norm_ref[...] = jnp.broadcast_to(norm, norm_ref.shape)


def row_norms(block, rows):
    return pl.pallas_call(
        norm_kernel,
        out_shape=jax.ShapeDtypeStruct((rows, LANES), jnp.float32),
        in_specs=[VMEM],
        out_specs=VMEM,
        cost_estimate=AHEAD,
        compiler_params=PARAMS,
    )(block)


def tile_kernel(places, normed, blocks, first, fixed_ref, *refs):
    count = len(places)
    texts, refs = refs[:count], refs[count:]
    norms, refs = dict(zip(normed, refs)), refs[len(normed) :]
    sums_ref, away_ref, keep_ref = refs[-1], refs[-2], refs[-3]
    grads, refs = refs[-3 - count : -3], refs[: -3 - count]
    if first:
        high_ref, low_ref, label_ref = refs[blocks:]
        image_units(refs[:blocks], high_ref, low_ref, label_ref)
        before = ()
    else:
        high_ref, low_ref, label_ref, *before = refs
    rows = grads[0].shape[0]
    total = high_ref.shape[0]
    scale, bias = fixed_ref[0:1, 0:1], fixed_ref[1:2, 0:1]
    labels = label_ref[0:1, :]
    sub = lax.rem(lax.broadcasted_iota(jnp.int32, (count * rows, total), 0), rows).astype(jnp.float32)
    wide = count * rows
    units = []
    for at in range(count):
        if at in norms:
            units.append(halves(unpack(texts[at], rows) / norms[at][:, 0:1]))
        else:
            units.append(halves(unit_rows(unpack(texts[at], rows))[0]))
    high = jnp.concatenate([unit[0] for unit in units], axis=0)
    low = jnp.concatenate([unit[1] for unit in units], axis=0)
    both = dot(jnp.concatenate([high, low], axis=0), high_ref[...], ((1,), (1,)))
    cosine = both[:wide] + (both[wide:] + dot(high, low_ref[...], ((1,), (1,))))
    logit = scale * cosine + bias
    starts = [jnp.broadcast_to(fixed_ref[2 + place : 3 + place, 0:1], (rows, 1)) for place in places]
    positive = sub + jnp.concatenate(starts, axis=0) == labels
    decay = jnp.exp(-jnp.abs(logit))
    term = jnp.maximum(jnp.where(positive, -logit, logit), 0.0) + jnp.log1p(decay)
    sigmoid = jnp.where(logit >= 0, 1.0, decay) / (1.0 + decay)
    slope = sigmoid - positive.astype(jnp.float32)
    parts = []
    for value in (term, slope, slope * cosine):
        row = jnp.sum(value, axis=0, keepdims=True)
        parts.append(functools.reduce(jnp.add, [row[:, at : at + LANES] for at in range(0, total, LANES)]))
    sums = jnp.concatenate(parts + [jnp.zeros((5, LANES), jnp.float32)], axis=0)
    slope_high, slope_low = halves(slope)
    both = dot(jnp.concatenate([slope_high, slope_low], axis=0), high_ref[...], ((1,), (0,)))
    both = both[:wide] + (both[wide:] + dot(slope_high, low_ref[...], ((1,), (0,))))
    for at in range(count):
        grads[at][...] = both[at * rows : (at + 1) * rows]
    slopes = jnp.concatenate([slope_high, slope_high, slope_low], axis=0)
    image = dot(slopes, jnp.concatenate([high, low, high], axis=0), ((0,), (0,)))
    half = total // 2
    if before:
        keep_ref[...] = before[0][...] + image[:half]
        away_ref[...] = before[1][...] + image[half:]
        sums_ref[...] = before[2][...] + sums
    else:
        keep_ref[...] = image[:half]
        away_ref[...] = image[half:]
        sums_ref[...] = sums


def tile(rows, width, places, fixed, texts, norms, blocks=(), before=()):
    count = len(texts)
    total = rows * len(blocks) if blocks else before[0].shape[0]
    normed = tuple(at for at, norm in enumerate(norms) if norm is not None)
    inputs = [fixed, *texts, *(norms[at] for at in normed), *blocks, *before]
    shapes = [jax.ShapeDtypeStruct((total, width), jnp.bfloat16)] * 2 if blocks else []
    shapes += [jax.ShapeDtypeStruct((8, total), jnp.float32)] if blocks else []
    units = len(shapes)
    shapes += [jax.ShapeDtypeStruct((rows, width), jnp.float32)] * count
    shapes += [jax.ShapeDtypeStruct((total // 2, width), jnp.float32)] * 2
    shapes += [jax.ShapeDtypeStruct((8, LANES), jnp.float32)]
    out = pl.pallas_call(
        functools.partial(tile_kernel, places, normed, len(blocks), bool(blocks)),
        out_shape=shapes,
        in_specs=[VMEM] * len(inputs),
        out_specs=[VMEM] * len(shapes),
        compiler_params=PARAMS,
    )(*inputs)
    return out[:units], out[units : units + count], out[-3:]


def join_kernel(count, *refs):
    parts, others, out_ref = refs[:count], refs[count:-1], refs[-1]
    total = functools.reduce(jnp.add, [part[...] for part in parts])
    if not others:
        out_ref[...] = total
        return
    rows, width = total.shape
    for at in range(0, width, LANES):
        out_ref[pl.ds(at // LANES * rows, rows), :] = total[:, at : at + LANES]
    out_ref[pl.ds(width // LANES * rows, 8), :] = others[0][...]


def join(parts, scalars=None, cost=None):
    rows, width = parts[0].shape
    others = [] if scalars is None else [scalars]
    shape = (rows, width) if scalars is None else (width // LANES * rows + 8, LANES)
    return pl.pallas_call(
        functools.partial(join_kernel, len(parts)),
        out_shape=jax.ShapeDtypeStruct(shape, jnp.float32),
        in_specs=[VMEM] * (len(parts) + len(others)),
        out_specs=VMEM,
        cost_estimate=cost,
        compiler_params=PARAMS,
    )(*parts, *others)


def final_kernel(pairs, counts, fixed_ref, sums_ref, *refs):
    scale = fixed_ref[0:1, 0:1]
    ins, (image_ref, text_ref, loss_ref, scale_ref, bias_ref) = refs[:-5], refs[-5:]
    sums = jnp.sum(sums_ref[0:3, :], axis=1, keepdims=True) * (1.0 / pairs)
    loss_ref[0] = sums[0, 0]
    bias_ref[0] = sums[1, 0]
    scale_ref[0] = (scale * sums[2:3, :])[0, 0]
    for own_ref, parts, out_ref in (
        (ins[0], ins[1 : 1 + counts[0]], image_ref),
        (ins[1 + counts[0]], ins[2 + counts[0] :], text_ref),
    ):
        total = functools.reduce(jnp.add, [part[...] for part in parts])
        grad = scale * total
        unit, norm = unit_rows(own_ref[...])
        out_ref[...] = (grad - unit * jnp.sum(unit * grad, axis=1, keepdims=True)) / norm


def final(pairs, fixed, scalars, image, image_parts, text, text_parts):
    counts = (len(image_parts), len(text_parts))
    return pl.pallas_call(
        functools.partial(final_kernel, pairs, counts),
        out_shape=[jax.ShapeDtypeStruct(image.shape, jnp.float32)] * 2
        + [jax.ShapeDtypeStruct((1,), jnp.float32)] * 3,
        in_specs=[VMEM] * (4 + sum(counts)),
        out_specs=[VMEM] * 2 + [SMEM] * 3,
        compiler_params=PARAMS,
    )(fixed, scalars, image, *image_parts, text, *text_parts)


def returns(steps):
    masks, order = [0], []
    for step in steps:
        order.insert(0, (step, [mask ^ step for mask in reversed(masks)]))
        masks += [mask ^ step for mask in masks]
    return order


def send_back(parts, step, masks, send):
    last = None
    for mask in masks:
        value = parts.pop(mask)
        value = value[0] if len(value) == 1 else join(value)
        last = send(value if last is None else after(value, last), step)
        parts[mask ^ step].append(last)


def per_device(count, image, text, labels, log_scale, bias):
    rows, width = image.shape
    pairs = rows * count
    me = lax.axis_index("row") * lax.axis_size("col") + lax.axis_index("col")
    image_steps, text_steps = generators(count)
    core = image_steps[-1]
    send = functools.partial(exchange, count=count)

    masks = [0]
    for step in text_steps:
        masks += [mask ^ step for mask in masks]
    fixed = constants(masks, rows, me.astype(jnp.int32).reshape(1), log_scale, bias)

    packed_image, packed_text = pack(image, text, labels)
    texts, norms = {0: packed_text}, {}
    for step in text_steps:
        far = list(texts)[1:]
        texts[step] = send(texts[0], step)
        for mask in far:
            norms[mask] = row_norms(texts[mask], rows)
            texts[mask ^ step] = send(after(texts[mask], norms[mask]), step)
    images = {0: packed_image}
    for step in image_steps[:-1]:
        far = list(images)[1:]
        images[step] = send(images[0], step)
        for mask in far:
            images[mask ^ step] = send(after(images[mask], fixed), step)
    near = list(images)
    for mask in near:
        block = images[mask]
        if mask == near[-1]:
            block = after(block, *norms.values(), *(texts[step] for step in text_steps))
        images[mask ^ core] = send(block, core)

    text_masks = list(texts)
    grads, units, sums = {}, (), ()
    for group in (text_masks[:-1], text_masks[-1:]):
        places = [masks.index(mask) for mask in group]
        arrays, known = [texts[mask] for mask in group], [norms.get(mask) for mask in group]
        blocks = () if units else list(images.values())
        made, parts, sums = tile(rows, width, places, fixed, arrays, known, blocks, [*units, *sums])
        units = units or made
        grads.update(zip(group, parts))
    keep, away, scalars = sums

    for step in text_steps[:0:-1]:
        scalars = join([scalars, send(scalars, step)], cost=AHEAD)
    near_sums = scalars
    scalars = scalars + send(scalars, core)
    scalars = join([scalars, send(scalars, text_steps[0])], cost=AHEAD)

    text_parts = {mask: [part] for mask, part in grads.items()}
    order = returns(text_steps)
    for step, masks in order[:-1]:
        send_back(text_parts, step, masks, send)
    far = join(text_parts.pop(text_steps[0]))
    scalars = after(scalars, far)
    text_parts[0].append(send(far, text_steps[0]))
    kept = keep + after(send(away, core), near_sums)
    image_parts = {mask: [kept[at * rows : (at + 1) * rows]] for at, mask in enumerate(near)}
    for step, masks in returns(image_steps[:-1]):
        send_back(image_parts, step, masks, send)
    for step in image_steps[:-1]:
        scalars = scalars + send(scalars, step)

    grad_image, grad_text, loss, grad_log_scale, grad_bias = final(
        pairs, fixed, scalars, image, image_parts[0], text, text_parts[0]
    )
    return (loss, grad_image, grad_text, grad_log_scale, grad_bias)


def solution(mesh):
    count = mesh.shape["row"] * mesh.shape["col"]
    return jax.shard_map(
        functools.partial(per_device, count),
        mesh=mesh,
        in_specs=(P(AXES, None), P(AXES, None), P(AXES), P(), P()),
        out_specs=(P(), P(AXES, None), P(AXES, None), P(), P()),
        check_vma=False,
    )
```

```python
import functools

import jax
import jax.numpy as jnp
from jax import lax
from jax.experimental import pallas as pl
from jax.experimental.pallas import tpu as pltpu
from jax.sharding import PartitionSpec as P

EPSILON = 1e-06
LANES = 128
PAD = 8
AXES = ("row", "col")
VMEM = pl.BlockSpec(memory_space=pltpu.VMEM)
SMEM = pl.BlockSpec(memory_space=pltpu.SMEM)
PARAMS = pltpu.CompilerParams(vmem_limit_bytes=40 << 20)
AHEAD = pl.CostEstimate(flops=10**10, bytes_accessed=10**10, transcendentals=0)


def generators(count):
    image, text = [], []
    for bit in range(1, count.bit_length() - 1):
        (text if bit in (2, 3) or bit > 4 and bit % 2 else image).append(1 << bit)
    return image + [1], text[::-1]


def exchange(value, step, count):
    return lax.ppermute(value, AXES, [(i, i ^ step) for i in range(count)])


def after(value, *others):
    return lax.optimization_barrier((value, *others))[0]


def unit_rows(rows):
    norm = jnp.sqrt(jnp.sum(rows * rows, axis=1, keepdims=True) + EPSILON)
    inverse = 1.0 / norm
    return rows * inverse, inverse


def halves(value):
    high = value.astype(jnp.bfloat16)
    low = (value - high.astype(jnp.float32)).astype(jnp.bfloat16)
    return high, low


def dot(left, right, dims):
    return lax.dot_general(left, right, (dims, ((), ())), preferred_element_type=jnp.float32)


def constants_kernel(masks, rows, me_ref, log_scale_ref, bias_ref, out_ref):
    values = [jnp.exp(jnp.full((1, LANES), log_scale_ref[0], jnp.float32))]
    values.append(jnp.full((1, LANES), bias_ref[0], jnp.float32))
    for mask in masks:
        first = jnp.bitwise_xor(me_ref[0], mask) * rows
        values.append(jnp.full((1, LANES), first, jnp.int32).astype(jnp.float32))
    values.append(jnp.zeros((out_ref.shape[0] - len(values), LANES), jnp.float32))
    out_ref[...] = jnp.concatenate(values, axis=0)


def constants(masks, rows, me, log_scale, bias):
    return pl.pallas_call(
        functools.partial(constants_kernel, masks, rows),
        out_shape=jax.ShapeDtypeStruct((len(masks) // 8 * 8 + 8, LANES), jnp.float32),
        in_specs=[SMEM] * 3,
        out_specs=VMEM,
        compiler_params=PARAMS,
    )(me, log_scale, bias)


def pack_kernel(image_ref, text_ref, label_ref, image_out, text_out, image, text, labels, sems):
    rows, width = image_ref.shape
    moves = [(text_ref, text), (image_ref, image), (label_ref, labels)]
    copies = [pltpu.make_async_copy(*move, sems.at[at]) for at, move in enumerate(moves)]
    for copy in copies:
        copy.start()
    text_out[pl.ds(width // LANES * rows, PAD), :] = jnp.zeros((PAD, LANES), jnp.float32)
    for copy, held, out in zip(copies, (text, image), (text_out, image_out)):
        copy.wait()
        for at in range(0, width, LANES):
            out[pl.ds(at // LANES * rows, rows), :] = held[:, pl.ds(at, LANES)]
    copies[2].wait()
    label = labels[...].astype(jnp.float32)
    image_out[pl.ds(width // LANES * rows, 1), :] = jnp.concatenate([label, label], axis=1)


def pack(image, text, labels):
    rows, width = image.shape
    pieces = width // LANES * rows
    return pl.pallas_call(
        pack_kernel,
        out_shape=[jax.ShapeDtypeStruct((pieces + more, LANES), jnp.float32) for more in (1, PAD)],
        in_specs=[pl.BlockSpec(memory_space=pltpu.HBM)] * 3,
        out_specs=[VMEM] * 2,
        scratch_shapes=[
            pltpu.VMEM((rows, width), jnp.float32),
            pltpu.VMEM((rows, width), jnp.float32),
            pltpu.VMEM((1, rows), jnp.int32),
            pltpu.SemaphoreType.DMA((3,)),
        ],
        compiler_params=pltpu.CompilerParams(vmem_limit_bytes=60 << 20),
    )(image, text, labels.reshape(1, rows))


def unpack(ref, rows):
    return jnp.concatenate([ref[pl.ds(at, rows), :] for at in range(0, ref.shape[0] // rows * rows, rows)], axis=1)


def image_units(blocks, high_ref, low_ref, label_ref):
    count = len(blocks)
    rows = high_ref.shape[0] // count
    width = high_ref.shape[1]
    for at, block in enumerate(blocks):
        squares = jnp.zeros((rows, LANES), jnp.float32)
        for piece in range(width // LANES):
            part = block[pl.ds(piece * rows, rows), :]
            squares += part * part
        inverse = 1.0 / jnp.sqrt(jnp.sum(squares, axis=1, keepdims=True) + EPSILON)
        for piece in range(width // LANES):
            high, low = halves(block[pl.ds(piece * rows, rows), :] * inverse)
            high_ref[pl.ds(at * rows, rows), pl.ds(piece * LANES, LANES)] = high
            low_ref[pl.ds(at * rows, rows), pl.ds(piece * LANES, LANES)] = low
    lane = lax.broadcasted_iota(jnp.int32, (1, LANES), 1)
    tail = pl.ds(width // LANES * rows, 1)
    for at in range(0, count, 2):
        pair = jnp.where(lane < rows, blocks[at][tail, :], blocks[at + 1][tail, :])
        label_ref[0:1, pl.ds(at * rows, LANES)] = pair


def norm_kernel(block_ref, norm_ref):
    block = unpack(block_ref, norm_ref.shape[0])
    norm = jnp.sqrt(jnp.sum(block * block, axis=1, keepdims=True) + EPSILON)
    norm_ref[...] = jnp.broadcast_to(1.0 / norm, norm_ref.shape)


def row_norms(block, rows):
    return pl.pallas_call(
        norm_kernel,
        out_shape=jax.ShapeDtypeStruct((rows, LANES), jnp.float32),
        in_specs=[VMEM],
        out_specs=VMEM,
        cost_estimate=AHEAD,
        compiler_params=PARAMS,
    )(block)


def tile_kernel(places, normed, blocks, first, fixed_ref, *refs):
    count = len(places)
    texts, refs = refs[:count], refs[count:]
    norms, refs = dict(zip(normed, refs)), refs[len(normed) :]
    sums_ref, away_ref, keep_ref = refs[-1], refs[-2], refs[-3]
    grads, refs = refs[-3 - count : -3], refs[: -3 - count]
    if first:
        high_ref, low_ref, label_ref = refs[blocks:]
        image_units(refs[:blocks], high_ref, low_ref, label_ref)
        before = ()
    else:
        high_ref, low_ref, label_ref, *before = refs
    rows = grads[0].shape[0]
    total = high_ref.shape[0]
    scale, bias = fixed_ref[0:1, 0:1], fixed_ref[1:2, 0:1]
    labels = label_ref[0:1, :]
    sub = lax.rem(lax.broadcasted_iota(jnp.int32, (count * rows, total), 0), rows).astype(jnp.float32)
    wide = count * rows
    units = []
    for at in range(count):
        if at in norms:
            units.append(halves(unpack(texts[at], rows) * norms[at][:, 0:1]))
        else:
            units.append(halves(unit_rows(unpack(texts[at], rows))[0]))
    high = jnp.concatenate([unit[0] for unit in units], axis=0)
    low = jnp.concatenate([unit[1] for unit in units], axis=0)
    both = dot(jnp.concatenate([high, low], axis=0), high_ref[...], ((1,), (1,)))
    cosine = both[:wide] + (both[wide:] + dot(high, low_ref[...], ((1,), (1,))))
    logit = scale * cosine + bias
    starts = [jnp.broadcast_to(fixed_ref[2 + place : 3 + place, 0:1], (rows, 1)) for place in places]
    positive = sub + jnp.concatenate(starts, axis=0) == labels
    decay = jnp.exp(-jnp.abs(logit))
    term = jnp.maximum(jnp.where(positive, -logit, logit), 0.0) + jnp.log1p(decay)
    sigmoid = jnp.where(logit >= 0, 1.0, decay) / (1.0 + decay)
    slope = sigmoid - positive.astype(jnp.float32)
    parts = []
    for value in (term, slope, slope * cosine):
        row = jnp.sum(value, axis=0, keepdims=True)
        parts.append(functools.reduce(jnp.add, [row[:, at : at + LANES] for at in range(0, total, LANES)]))
    sums = jnp.concatenate(parts + [jnp.zeros((5, LANES), jnp.float32)], axis=0)
    slope_high, slope_low = halves(slope)
    both = dot(jnp.concatenate([slope_high, slope_low], axis=0), high_ref[...], ((1,), (0,)))
    both = both[:wide] + (both[wide:] + dot(slope_high, low_ref[...], ((1,), (0,))))
    for at in range(count):
        grads[at][...] = both[at * rows : (at + 1) * rows]
    slopes = jnp.concatenate([slope_high, slope_high, slope_low], axis=0)
    image = dot(slopes, jnp.concatenate([high, low, high], axis=0), ((0,), (0,)))
    half = total // 2
    if before:
        keep_ref[...] = before[0][...] + image[:half]
        away_ref[...] = before[1][...] + image[half:]
        sums_ref[...] = before[2][...] + sums
    else:
        keep_ref[...] = image[:half]
        away_ref[...] = image[half:]
        sums_ref[...] = sums


def tile(rows, width, places, fixed, texts, norms, blocks=(), before=()):
    count = len(texts)
    total = rows * len(blocks) if blocks else before[0].shape[0]
    normed = tuple(at for at, norm in enumerate(norms) if norm is not None)
    inputs = [fixed, *texts, *(norms[at] for at in normed), *blocks, *before]
    shapes = [jax.ShapeDtypeStruct((total, width), jnp.bfloat16)] * 2 if blocks else []
    shapes += [jax.ShapeDtypeStruct((8, total), jnp.float32)] if blocks else []
    units = len(shapes)
    shapes += [jax.ShapeDtypeStruct((rows, width), jnp.float32)] * count
    shapes += [jax.ShapeDtypeStruct((total // 2, width), jnp.float32)] * 2
    shapes += [jax.ShapeDtypeStruct((8, LANES), jnp.float32)]
    out = pl.pallas_call(
        functools.partial(tile_kernel, places, normed, len(blocks), bool(blocks)),
        out_shape=shapes,
        in_specs=[VMEM] * len(inputs),
        out_specs=[VMEM] * len(shapes),
        compiler_params=PARAMS,
    )(*inputs)
    return out[:units], out[units : units + count], out[-3:]


def join_kernel(count, *refs):
    parts, others, out_ref = refs[:count], refs[count:-1], refs[-1]
    total = functools.reduce(jnp.add, [part[...] for part in parts])
    if not others:
        out_ref[...] = total
        return
    rows, width = total.shape
    for at in range(0, width, LANES):
        out_ref[pl.ds(at // LANES * rows, rows), :] = total[:, at : at + LANES]
    out_ref[pl.ds(width // LANES * rows, 8), :] = others[0][...]


def join(parts, scalars=None, cost=None):
    rows, width = parts[0].shape
    others = [] if scalars is None else [scalars]
    shape = (rows, width) if scalars is None else (width // LANES * rows + 8, LANES)
    return pl.pallas_call(
        functools.partial(join_kernel, len(parts)),
        out_shape=jax.ShapeDtypeStruct(shape, jnp.float32),
        in_specs=[VMEM] * (len(parts) + len(others)),
        out_specs=VMEM,
        cost_estimate=cost,
        compiler_params=PARAMS,
    )(*parts, *others)


def final_kernel(pairs, counts, fixed_ref, sums_ref, *refs):
    scale = fixed_ref[0:1, 0:1]
    ins, (image_ref, text_ref, loss_ref, scale_ref, bias_ref) = refs[:-5], refs[-5:]
    sums = jnp.sum(sums_ref[0:3, :], axis=1, keepdims=True) * (1.0 / pairs)
    loss_ref[0] = sums[0, 0]
    bias_ref[0] = sums[1, 0]
    scale_ref[0] = (scale * sums[2:3, :])[0, 0]
    for own_ref, parts, out_ref in (
        (ins[0], ins[1 : 1 + counts[0]], image_ref),
        (ins[1 + counts[0]], ins[2 + counts[0] :], text_ref),
    ):
        total = functools.reduce(jnp.add, [part[...] for part in parts])
        grad = scale * total
        unit, inverse = unit_rows(own_ref[...])
        out_ref[...] = (grad - unit * jnp.sum(unit * grad, axis=1, keepdims=True)) * inverse


def final(pairs, fixed, scalars, image, image_parts, text, text_parts):
    counts = (len(image_parts), len(text_parts))
    return pl.pallas_call(
        functools.partial(final_kernel, pairs, counts),
        out_shape=[jax.ShapeDtypeStruct(image.shape, jnp.float32)] * 2
        + [jax.ShapeDtypeStruct((1,), jnp.float32)] * 3,
        in_specs=[VMEM] * (4 + sum(counts)),
        out_specs=[VMEM] * 2 + [SMEM] * 3,
        compiler_params=PARAMS,
    )(fixed, scalars, image, *image_parts, text, *text_parts)


def returns(steps):
    masks, order = [0], []
    for step in steps:
        order.insert(0, (step, [mask ^ step for mask in reversed(masks)]))
        masks += [mask ^ step for mask in masks]
    return order


def send_back(parts, step, masks, send):
    last = None
    for mask in masks:
        value = parts.pop(mask)
        value = value[0] if len(value) == 1 else join(value)
        last = send(value if last is None else after(value, last), step)
        parts[mask ^ step].append(last)


def per_device(count, image, text, labels, log_scale, bias):
    rows, width = image.shape
    pairs = rows * count
    me = lax.axis_index("row") * lax.axis_size("col") + lax.axis_index("col")
    image_steps, text_steps = generators(count)
    core = image_steps[-1]
    send = functools.partial(exchange, count=count)

    masks = [0]
    for step in text_steps:
        masks += [mask ^ step for mask in masks]
    fixed = constants(masks, rows, me.astype(jnp.int32).reshape(1), log_scale, bias)

    packed_image, packed_text = pack(image, text, labels)
    texts, norms = {0: packed_text}, {}
    for step in text_steps:
        far = list(texts)[1:]
        texts[step] = send(texts[0], step)
        for mask in far:
            norms[mask] = row_norms(texts[mask], rows)
            texts[mask ^ step] = send(after(texts[mask], norms[mask]), step)
    images = {0: packed_image}
    for step in image_steps[:-1]:
        far = list(images)[1:]
        images[step] = send(images[0], step)
        for mask in far:
            images[mask ^ step] = send(after(images[mask], fixed), step)
    near = list(images)
    for mask in near:
        block = images[mask]
        if mask == near[-1]:
            block = after(block, *norms.values(), *(texts[step] for step in text_steps))
        images[mask ^ core] = send(block, core)

    text_masks = list(texts)
    grads, units, sums = {}, (), ()
    for group in (text_masks[:-1], text_masks[-1:]):
        places = [masks.index(mask) for mask in group]
        arrays, known = [texts[mask] for mask in group], [norms.get(mask) for mask in group]
        blocks = () if units else list(images.values())
        made, parts, sums = tile(rows, width, places, fixed, arrays, known, blocks, [*units, *sums])
        units = units or made
        grads.update(zip(group, parts))
    keep, away, scalars = sums

    for step in text_steps[:0:-1]:
        scalars = join([scalars, send(scalars, step)], cost=AHEAD)
    near_sums = scalars
    scalars = scalars + send(scalars, core)
    scalars = join([scalars, send(scalars, text_steps[0])], cost=AHEAD)

    text_parts = {mask: [part] for mask, part in grads.items()}
    order = returns(text_steps)
    for step, masks in order[:-1]:
        send_back(text_parts, step, masks, send)
    far = join(text_parts.pop(text_steps[0]))
    scalars = after(scalars, far)
    text_parts[0].append(send(far, text_steps[0]))
    kept = keep + after(send(away, core), near_sums)
    image_parts = {mask: [kept[at * rows : (at + 1) * rows]] for at, mask in enumerate(near)}
    for step, masks in returns(image_steps[:-1]):
        send_back(image_parts, step, masks, send)
    for step in image_steps[:-1]:
        scalars = scalars + send(scalars, step)

    grad_image, grad_text, loss, grad_log_scale, grad_bias = final(
        pairs, fixed, scalars, image, image_parts[0], text, text_parts[0]
    )
    return (loss, grad_image, grad_text, grad_log_scale, grad_bias)


def solution(mesh):
    count = mesh.shape["row"] * mesh.shape["col"]
    return jax.shard_map(
        functools.partial(per_device, count),
        mesh=mesh,
        in_specs=(P(AXES, None), P(AXES, None), P(AXES), P(), P()),
        out_specs=(P(), P(AXES, None), P(AXES, None), P(), P()),
        check_vma=False,
    )
```

```python
import functools

import jax
import jax.numpy as jnp
from jax import lax
from jax.experimental import pallas as pl
from jax.experimental.pallas import tpu as pltpu
from jax.sharding import PartitionSpec as P

EPSILON = 1e-06
LANES = 128
PAD = 8
AXES = ("row", "col")
VMEM = pl.BlockSpec(memory_space=pltpu.VMEM)
SMEM = pl.BlockSpec(memory_space=pltpu.SMEM)
PARAMS = pltpu.CompilerParams(vmem_limit_bytes=40 << 20)
AHEAD = pl.CostEstimate(flops=10**10, bytes_accessed=10**10, transcendentals=0)


def generators(count):
    image, text = [], []
    for bit in range(1, count.bit_length() - 1):
        (text if bit in (2, 3) or bit > 4 and bit % 2 else image).append(1 << bit)
    return image[::-1] + [1], text[::-1]


def exchange(value, step, count):
    return lax.ppermute(value, AXES, [(i, i ^ step) for i in range(count)])


def after(value, *others):
    return lax.optimization_barrier((value, *others))[0]


def unit_rows(rows):
    norm = jnp.sqrt(jnp.sum(rows * rows, axis=1, keepdims=True) + EPSILON)
    return rows / norm, norm


def halves(value):
    high = value.astype(jnp.bfloat16)
    low = (value - high.astype(jnp.float32)).astype(jnp.bfloat16)
    return high, low


def dot(left, right, dims):
    return lax.dot_general(left, right, (dims, ((), ())), preferred_element_type=jnp.float32)


def constants_kernel(masks, rows, me_ref, log_scale_ref, bias_ref, out_ref):
    values = [jnp.exp(jnp.full((1, LANES), log_scale_ref[0], jnp.float32))]
    values.append(jnp.full((1, LANES), bias_ref[0], jnp.float32))
    for mask in masks:
        first = jnp.bitwise_xor(me_ref[0], mask) * rows
        values.append(jnp.full((1, LANES), first, jnp.int32).astype(jnp.float32))
    values.append(jnp.zeros((out_ref.shape[0] - len(values), LANES), jnp.float32))
    out_ref[...] = jnp.concatenate(values, axis=0)


def constants(masks, rows, me, log_scale, bias):
    return pl.pallas_call(
        functools.partial(constants_kernel, masks, rows),
        out_shape=jax.ShapeDtypeStruct((len(masks) // 8 * 8 + 8, LANES), jnp.float32),
        in_specs=[SMEM] * 3,
        out_specs=VMEM,
        compiler_params=PARAMS,
    )(me, log_scale, bias)


def pack_kernel(image_ref, text_ref, label_ref, image_out, text_out, image, text, labels, sems):
    rows, width = image_ref.shape
    moves = [(text_ref, text), (image_ref, image), (label_ref, labels)]
    copies = [pltpu.make_async_copy(*move, sems.at[at]) for at, move in enumerate(moves)]
    for copy in copies:
        copy.start()
    text_out[pl.ds(width // LANES * rows, PAD), :] = jnp.zeros((PAD, LANES), jnp.float32)
    for copy, held, out in zip(copies, (text, image), (text_out, image_out)):
        copy.wait()
        for at in range(0, width, LANES):
            out[pl.ds(at // LANES * rows, rows), :] = held[:, pl.ds(at, LANES)]
    copies[2].wait()
    label = labels[...].astype(jnp.float32)
    image_out[pl.ds(width // LANES * rows, 1), :] = jnp.concatenate([label, label], axis=1)


def pack(image, text, labels):
    rows, width = image.shape
    pieces = width // LANES * rows
    return pl.pallas_call(
        pack_kernel,
        out_shape=[jax.ShapeDtypeStruct((pieces + more, LANES), jnp.float32) for more in (1, PAD)],
        in_specs=[pl.BlockSpec(memory_space=pltpu.HBM)] * 3,
        out_specs=[VMEM] * 2,
        scratch_shapes=[
            pltpu.VMEM((rows, width), jnp.float32),
            pltpu.VMEM((rows, width), jnp.float32),
            pltpu.VMEM((1, rows), jnp.int32),
            pltpu.SemaphoreType.DMA((3,)),
        ],
        compiler_params=pltpu.CompilerParams(vmem_limit_bytes=60 << 20),
    )(image, text, labels.reshape(1, rows))


def unpack(ref, rows):
    return jnp.concatenate([ref[pl.ds(at, rows), :] for at in range(0, ref.shape[0] // rows * rows, rows)], axis=1)


def image_units(blocks, high_ref, low_ref, label_ref):
    count = len(blocks)
    rows = high_ref.shape[0] // count
    width = high_ref.shape[1]
    for at, block in enumerate(blocks):
        squares = jnp.zeros((rows, LANES), jnp.float32)
        for piece in range(width // LANES):
            part = block[pl.ds(piece * rows, rows), :]
            squares += part * part
        norm = jnp.sqrt(jnp.sum(squares, axis=1, keepdims=True) + EPSILON)
        for piece in range(width // LANES):
            high, low = halves(block[pl.ds(piece * rows, rows), :] / norm)
            high_ref[pl.ds(at * rows, rows), pl.ds(piece * LANES, LANES)] = high
            low_ref[pl.ds(at * rows, rows), pl.ds(piece * LANES, LANES)] = low
    lane = lax.broadcasted_iota(jnp.int32, (1, LANES), 1)
    tail = pl.ds(width // LANES * rows, 1)
    for at in range(0, count, 2):
        pair = jnp.where(lane < rows, blocks[at][tail, :], blocks[at + 1][tail, :])
        label_ref[0:1, pl.ds(at * rows, LANES)] = pair


def norm_kernel(block_ref, norm_ref):
    block = unpack(block_ref, norm_ref.shape[0])
    norm = jnp.sqrt(jnp.sum(block * block, axis=1, keepdims=True) + EPSILON)
    norm_ref[...] = jnp.broadcast_to(norm, norm_ref.shape)


def row_norms(block, rows):
    return pl.pallas_call(
        norm_kernel,
        out_shape=jax.ShapeDtypeStruct((rows, LANES), jnp.float32),
        in_specs=[VMEM],
        out_specs=VMEM,
        cost_estimate=AHEAD,
        compiler_params=PARAMS,
    )(block)


def tile_kernel(places, normed, blocks, first, fixed_ref, *refs):
    count = len(places)
    texts, refs = refs[:count], refs[count:]
    norms, refs = dict(zip(normed, refs)), refs[len(normed) :]
    sums_ref, away_ref, keep_ref = refs[-1], refs[-2], refs[-3]
    grads, refs = refs[-3 - count : -3], refs[: -3 - count]
    if first:
        high_ref, low_ref, label_ref = refs[blocks:]
        image_units(refs[:blocks], high_ref, low_ref, label_ref)
        before = ()
    else:
        high_ref, low_ref, label_ref, *before = refs
    rows = grads[0].shape[0]
    total = high_ref.shape[0]
    scale, bias = fixed_ref[0:1, 0:1], fixed_ref[1:2, 0:1]
    labels = label_ref[0:1, :]
    sub = lax.rem(lax.broadcasted_iota(jnp.int32, (count * rows, total), 0), rows).astype(jnp.float32)
    wide = count * rows
    units = []
    for at in range(count):
        if at in norms:
            units.append(halves(unpack(texts[at], rows) / norms[at][:, 0:1]))
        else:
            units.append(halves(unit_rows(unpack(texts[at], rows))[0]))
    high = jnp.concatenate([unit[0] for unit in units], axis=0)
    low = jnp.concatenate([unit[1] for unit in units], axis=0)
    both = dot(jnp.concatenate([high, low], axis=0), high_ref[...], ((1,), (1,)))
    cosine = both[:wide] + (both[wide:] + dot(high, low_ref[...], ((1,), (1,))))
    logit = scale * cosine + bias
    starts = [jnp.broadcast_to(fixed_ref[2 + place : 3 + place, 0:1], (rows, 1)) for place in places]
    positive = sub + jnp.concatenate(starts, axis=0) == labels
    decay = jnp.exp(-jnp.abs(logit))
    term = jnp.maximum(jnp.where(positive, -logit, logit), 0.0) + jnp.log1p(decay)
    sigmoid = jnp.where(logit >= 0, 1.0, decay) / (1.0 + decay)
    slope = sigmoid - positive.astype(jnp.float32)
    parts = []
    for value in (term, slope, slope * cosine):
        row = jnp.sum(value, axis=0, keepdims=True)
        parts.append(functools.reduce(jnp.add, [row[:, at : at + LANES] for at in range(0, total, LANES)]))
    sums = jnp.concatenate(parts + [jnp.zeros((5, LANES), jnp.float32)], axis=0)
    slope_high, slope_low = halves(slope)
    both = dot(jnp.concatenate([slope_high, slope_low], axis=0), high_ref[...], ((1,), (0,)))
    both = both[:wide] + (both[wide:] + dot(slope_high, low_ref[...], ((1,), (0,))))
    for at in range(count):
        grads[at][...] = both[at * rows : (at + 1) * rows]
    slopes = jnp.concatenate([slope_high, slope_high, slope_low], axis=0)
    image = dot(slopes, jnp.concatenate([high, low, high], axis=0), ((0,), (0,)))
    half = total // 2
    if before:
        keep_ref[...] = before[0][...] + image[:half]
        away_ref[...] = before[1][...] + image[half:]
        sums_ref[...] = before[2][...] + sums
    else:
        keep_ref[...] = image[:half]
        away_ref[...] = image[half:]
        sums_ref[...] = sums


def tile(rows, width, places, fixed, texts, norms, blocks=(), before=()):
    count = len(texts)
    total = rows * len(blocks) if blocks else before[0].shape[0]
    normed = tuple(at for at, norm in enumerate(norms) if norm is not None)
    inputs = [fixed, *texts, *(norms[at] for at in normed), *blocks, *before]
    shapes = [jax.ShapeDtypeStruct((total, width), jnp.bfloat16)] * 2 if blocks else []
    shapes += [jax.ShapeDtypeStruct((8, total), jnp.float32)] if blocks else []
    units = len(shapes)
    shapes += [jax.ShapeDtypeStruct((rows, width), jnp.float32)] * count
    shapes += [jax.ShapeDtypeStruct((total // 2, width), jnp.float32)] * 2
    shapes += [jax.ShapeDtypeStruct((8, LANES), jnp.float32)]
    out = pl.pallas_call(
        functools.partial(tile_kernel, places, normed, len(blocks), bool(blocks)),
        out_shape=shapes,
        in_specs=[VMEM] * len(inputs),
        out_specs=[VMEM] * len(shapes),
        compiler_params=PARAMS,
    )(*inputs)
    return out[:units], out[units : units + count], out[-3:]


def join_kernel(count, *refs):
    parts, others, out_ref = refs[:count], refs[count:-1], refs[-1]
    total = functools.reduce(jnp.add, [part[...] for part in parts])
    if not others:
        out_ref[...] = total
        return
    rows, width = total.shape
    for at in range(0, width, LANES):
        out_ref[pl.ds(at // LANES * rows, rows), :] = total[:, at : at + LANES]
    out_ref[pl.ds(width // LANES * rows, 8), :] = others[0][...]


def join(parts, scalars=None, cost=None):
    rows, width = parts[0].shape
    others = [] if scalars is None else [scalars]
    shape = (rows, width) if scalars is None else (width // LANES * rows + 8, LANES)
    return pl.pallas_call(
        functools.partial(join_kernel, len(parts)),
        out_shape=jax.ShapeDtypeStruct(shape, jnp.float32),
        in_specs=[VMEM] * (len(parts) + len(others)),
        out_specs=VMEM,
        cost_estimate=cost,
        compiler_params=PARAMS,
    )(*parts, *others)


def final_kernel(pairs, counts, fixed_ref, sums_ref, *refs):
    scale = fixed_ref[0:1, 0:1]
    ins, (image_ref, text_ref, loss_ref, scale_ref, bias_ref) = refs[:-5], refs[-5:]
    sums = jnp.sum(sums_ref[0:3, :], axis=1, keepdims=True) * (1.0 / pairs)
    loss_ref[0] = sums[0, 0]
    bias_ref[0] = sums[1, 0]
    scale_ref[0] = (scale * sums[2:3, :])[0, 0]
    for own_ref, parts, out_ref in (
        (ins[0], ins[1 : 1 + counts[0]], image_ref),
        (ins[1 + counts[0]], ins[2 + counts[0] :], text_ref),
    ):
        total = functools.reduce(jnp.add, [part[...] for part in parts])
        grad = scale * total
        unit, norm = unit_rows(own_ref[...])
        out_ref[...] = (grad - unit * jnp.sum(unit * grad, axis=1, keepdims=True)) / norm


def final(pairs, fixed, scalars, image, image_parts, text, text_parts):
    counts = (len(image_parts), len(text_parts))
    return pl.pallas_call(
        functools.partial(final_kernel, pairs, counts),
        out_shape=[jax.ShapeDtypeStruct(image.shape, jnp.float32)] * 2
        + [jax.ShapeDtypeStruct((1,), jnp.float32)] * 3,
        in_specs=[VMEM] * (4 + sum(counts)),
        out_specs=[VMEM] * 2 + [SMEM] * 3,
        compiler_params=PARAMS,
    )(fixed, scalars, image, *image_parts, text, *text_parts)


def returns(steps):
    masks, order = [0], []
    for step in steps:
        order.insert(0, (step, [mask ^ step for mask in reversed(masks)]))
        masks += [mask ^ step for mask in masks]
    return order


def send_back(parts, step, masks, send):
    last = None
    for mask in masks:
        value = parts.pop(mask)
        value = value[0] if len(value) == 1 else join(value)
        last = send(value if last is None else after(value, last), step)
        parts[mask ^ step].append(last)


def per_device(count, image, text, labels, log_scale, bias):
    rows, width = image.shape
    pairs = rows * count
    me = lax.axis_index("row") * lax.axis_size("col") + lax.axis_index("col")
    image_steps, text_steps = generators(count)
    core = image_steps[-1]
    send = functools.partial(exchange, count=count)

    masks = [0]
    for step in text_steps:
        masks += [mask ^ step for mask in masks]
    fixed = constants(masks, rows, me.astype(jnp.int32).reshape(1), log_scale, bias)

    packed_image, packed_text = pack(image, text, labels)
    texts, norms = {0: packed_text}, {}
    for step in text_steps:
        far = list(texts)[1:]
        texts[step] = send(texts[0], step)
        for mask in far:
            norms[mask] = row_norms(texts[mask], rows)
            texts[mask ^ step] = send(after(texts[mask], norms[mask]), step)
    images = {0: packed_image}
    for step in image_steps[:-1]:
        far = list(images)[1:]
        images[step] = send(images[0], step)
        for mask in far:
            images[mask ^ step] = send(after(images[mask], fixed), step)
    near = list(images)
    for mask in near:
        block = images[mask]
        if mask == near[-1]:
            block = after(block, *norms.values(), *(texts[step] for step in text_steps))
        images[mask ^ core] = send(block, core)

    text_masks = list(texts)
    grads, units, sums = {}, (), ()
    for group in (text_masks[:-1], text_masks[-1:]):
        places = [masks.index(mask) for mask in group]
        arrays, known = [texts[mask] for mask in group], [norms.get(mask) for mask in group]
        blocks = () if units else list(images.values())
        made, parts, sums = tile(rows, width, places, fixed, arrays, known, blocks, [*units, *sums])
        units = units or made
        grads.update(zip(group, parts))
    keep, away, scalars = sums

    for step in text_steps[:0:-1]:
        scalars = join([scalars, send(scalars, step)], cost=AHEAD)
    near_sums = scalars
    scalars = scalars + send(scalars, core)
    scalars = join([scalars, send(scalars, text_steps[0])], cost=AHEAD)

    text_parts = {mask: [part] for mask, part in grads.items()}
    order = returns(text_steps)
    for step, masks in order[:-1]:
        send_back(text_parts, step, masks, send)
    far = join(text_parts.pop(text_steps[0]))
    scalars = after(scalars, far)
    text_parts[0].append(send(far, text_steps[0]))
    kept = keep + after(send(away, core), near_sums)
    image_parts = {mask: [kept[at * rows : (at + 1) * rows]] for at, mask in enumerate(near)}
    for step, masks in returns(image_steps[:-1]):
        send_back(image_parts, step, masks, send)
    for step in image_steps[:-1]:
        scalars = scalars + send(scalars, step)

    grad_image, grad_text, loss, grad_log_scale, grad_bias = final(
        pairs, fixed, scalars, image, image_parts[0], text, text_parts[0]
    )
    return (loss, grad_image, grad_text, grad_log_scale, grad_bias)


def solution(mesh):
    count = mesh.shape["row"] * mesh.shape["col"]
    return jax.shard_map(
        functools.partial(per_device, count),
        mesh=mesh,
        in_specs=(P(AXES, None), P(AXES, None), P(AXES), P(), P()),
        out_specs=(P(), P(AXES, None), P(AXES, None), P(), P()),
        check_vma=False,
    )
```
